32 devices in a mesh: group: 2 (over y), space: 8 (over z, core), member: 2 (over x), level: 1.
Axes of the slice: x: 2, y: 2, z: 4, core: 2. Of those that a mesh axis runs over, the one named last changes fastest.
Arguments:
- atm_state: bfloat16 [2, 256, 128, 128], P('member', ('group', 'space')), parts along dimension 1, may hold values from -6 to 6
- remap_tiles: bfloat16 [128, 4, 128, 128], P('space'), may hold values from -0.375 to 0.375
- dest_device: int32 [128, 4], P('space'), may hold values from 0 to 7, all different within a row; in each aligned block of 16 rows (0 to 15, 16 to 31, ...) at most 16 rows name the same one
- dest_block: int32 [128, 4], P('space'), may hold values from 0 to 31
- wet_mask: int32 [256, 128], P('space'), may hold values 0 or 1
- target: float32 [2, 512, 4, 128], P('member', ('group', 'space')), parts along dimension 1, may hold values from -6 to 6
- w_in: bfloat16 [128, 1024], P(None, 'level'), may hold values from -0.5 to 0.5
- w_out: bfloat16 [1024, 4], P('level'), may hold values from -0.375 to 0.375
Outputs:
- atm_adjoint: float32 [2, 256, 128, 128], P('member', ('group', 'space'), 'level'), parts along dimension 1
- grad_w_in: float32 [256, 1024], P('group', 'level'), parts along dimension 0
- grad_w_out: float32 [1024, 8], P('level', 'group'), parts along dimension 1
The draws below stay inside these ranges and needn't reach their ends.
There are 2 independent parts, one for each index of `group`. The reference program is written for one: setup_inputs(seed, part) draws one part's arguments, and reference() takes and returns one part's arrays. A program takes and returns all parts, laid end to end along the dimension named above; an argument that names none is the same for every part. Nothing has to cross between parts.
Inputs may be any that keep to these rules, and one draw needn't show every extreme that they name: `dest_device`: among the 16 atmosphere blocks of one device, no owner is named more than 16 times, a bound that some block reaches; the 4 owners of one block are distinct.
All inputs are finite; a program needn't handle non-finite values. No bound on the sum of `wet_mask` on one device may be relied on, other than what follows from the above.
Results may differ from the reference program's by a relative error of at most 0.002.
The reference program's roundings to bfloat16 on the way (of `pieces`, `features`, `activated`, `pre_grad` and `feat_grad`) count: a program that leaves them out, or rounds other values in their place, can miss the bound.
Values may be sent and summed in bfloat16 or wider, within the bound.
A program may use at most 64 MiB of HBM per device.

```python
import math
import jax
import jax.numpy as jnp
import numpy as np
from jax import lax

C = 128
HID = 1024
Q = 4
BLK = 128
TOP = 4
ABLK_DEV = 16
OBLK_DEV = 32
MEMBERS = 2
A_BLOCKS = 128
O_BLOCKS = 256
CAP = 16
N_SPACE = 8


def place_ends(result, stream_key, smallest, top_value):
    spot = [jax.random.randint(jax.random.fold_in(stream_key, axis), (), 0, length) for axis, length in enumerate(result.shape)]
    longest = result.shape.index(max(result.shape))
    beside = spot[:longest] + [(spot[longest] + 1) % result.shape[longest]] + spot[longest + 1:]
    return result.at[tuple(spot)].set(smallest).at[tuple(beside)].set(top_value)


def shard_levels(key, extent, cuts, low, high):
    factor_of = 1.0
    for axis_at, parts in cuts:
        draws = jax.random.uniform(jax.random.fold_in(jax.random.fold_in(key, 6), axis_at), (parts,), jnp.float32, low / len(cuts), high / len(cuts))
        factor_of = factor_of * jnp.repeat(jnp.exp(draws), extent[axis_at] // parts).reshape((-1,) + (1,) * (len(extent) - 1 - axis_at))
    return factor_of


def routed_block(stream_key, own, number, rows, amount, top, bound, skew):
    ranking = jax.random.permutation(stream_key, amount)
    heavy_load, common = load_shares(amount, rows * top, bound, skew, True), load_shares(amount, rows * top, bound, skew, False)
    places = jnp.arange(amount)

    def named(sizes, rotation):
        used = int((sizes > 0).sum())
        fixed = max(1, used // 4)
        passed = fixed + (places - fixed + rotation * (used - fixed)) % max(1, amount - fixed)
        return jnp.zeros((amount,), jnp.int32).at[ranking[jnp.where(places < fixed, places, passed)]].set(jnp.asarray(sizes, jnp.int32))

    sizes = jnp.where(number % 4 == 0, named(heavy_load, number // 4), named(common, number - number // 4 - 1))
    mixed = jax.random.permutation(jax.random.fold_in(own, 3), amount)
    donor, receiver = mixed[0:amount // 2 * 2:2], mixed[1:amount // 2 * 2:2]
    room = jnp.minimum(sizes[donor] - 1, bound - sizes[receiver]) // 2
    room = jnp.where((donor == ranking[0]) | (receiver == ranking[0]) | (sizes[receiver] == 0), 0, jnp.maximum(room, 0))
    passed = jax.random.randint(jax.random.fold_in(own, 4), (amount // 2,), 0, 1 << 20) % (room + 1)
    sizes = sizes.at[donor].add(-passed).at[receiver].add(passed)
    members = jnp.searchsorted(jnp.cumsum(sizes), jnp.arange(rows * top), side="right").astype(jnp.int32)
    table = members.reshape(top, rows).T
    table = table[jax.random.permutation(jax.random.fold_in(own, 1), rows)]
    rotation = jax.random.randint(jax.random.fold_in(own, 2), (rows, 1), 0, top)
    return jnp.take_along_axis(table, (jnp.arange(top)[None, :] + rotation) % top, axis=1)


def load_shares(number_of, total, most, skew, full):
    loads = [(1 << 20) // math.isqrt(standing ** skew) + 1 for standing in range(1, number_of + 1)]
    largest = most if full else min(most, max(-(-total // number_of), total * loads[0] // sum(loads)))
    least = 1 if total - largest >= number_of - 1 else 0
    given, spare = [largest] + [least] * (number_of - 1), total - largest - least * (number_of - 1)
    while spare > 0:
        movable = [i for i in range(1, number_of) if given[i] < largest] or [i for i in range(1, number_of) if given[i] < most]
        whole, left = sum([loads[i] for i in movable]), spare
        for i in movable:
            more = min(most - given[i], max(1, left * loads[i] // whole), spare)
            given[i] = given[i] + more
            spare = spare - more
    return np.array(given)


def noise(stream_key, extent, deviation, reach, shards=(), held_as=jnp.bfloat16):
    drawn = jax.random.normal(stream_key, extent, jnp.float32) * deviation
    if len(shards) > 0:
        drawn = shard_levels(stream_key, extent, shards, -0.22, 0.18) * drawn
    return jnp.clip(drawn, min=-reach, max=reach).astype(held_as)


def setup_inputs(seed: int = 0, part: int = 0) -> dict:
    key_of = jax.random.split(jax.random.key(seed), 9)
    part_splits = jax.random.split(jax.random.fold_in(key_of[8], part), 9)
    atm_state = noise(part_splits[0], (MEMBERS, A_BLOCKS, C, BLK), 1.0, 6.0, ((0, 2), (1, 8)))
    remap_tiles = noise(key_of[1], (A_BLOCKS, TOP, BLK, BLK), (2 * BLK) ** -0.5, 0.375, ((0, 8),))
    dest_device_keys = jax.random.split(jax.random.fold_in(key_of[2], 1), A_BLOCKS // ABLK_DEV)
    dest_device_turns = jax.random.permutation(jax.random.fold_in(key_of[2], 3), A_BLOCKS // ABLK_DEV)
    dest_device = jax.vmap(lambda own, number: routed_block(jax.random.fold_in(key_of[2], 2), own, number, ABLK_DEV, N_SPACE, TOP, CAP, 2))(dest_device_keys, dest_device_turns).reshape((A_BLOCKS, TOP))
    dest_block = place_ends(jax.random.randint(key_of[3], (A_BLOCKS, TOP), 0, OBLK_DEV), jax.random.fold_in(key_of[3], 1), 0, OBLK_DEV - 1).astype(jnp.int32)
    wet_mask = place_ends((jax.random.randint(key_of[4], (O_BLOCKS, BLK), 0, 4) < 3).astype(jnp.int32), jax.random.fold_in(key_of[4], 1), 0, 1)
    target = noise(part_splits[5], (MEMBERS, O_BLOCKS, Q, BLK), 1.0, 6.0, ((0, 2), (1, 8)), jnp.float32)
    w_in = noise(key_of[6], (C, HID), C ** -0.5, 0.5)
    w_out = noise(key_of[7], (HID, Q), (HID // 4) ** -0.5, 0.375)
    return {"atm_state": atm_state, "remap_tiles": remap_tiles, "dest_device": dest_device, "dest_block": dest_block, "wet_mask": wet_mask, "target": target, "w_in": w_in, "w_out": w_out}


def reference(atm_state, remap_tiles, dest_device, dest_block, wet_mask, target, w_in, w_out):
    owner_block = (dest_device * OBLK_DEV + dest_block).reshape(-1).astype(jnp.int32)
    wet_cells = wet_mask.astype(jnp.float32)
    w_out_wide = w_out.astype(jnp.float32)
    tiles_wide = remap_tiles.astype(jnp.float32)
    cell_total = MEMBERS * O_BLOCKS * BLK
    scale_in = math.sqrt(HID / cell_total)
    scale_out = 1.0 / math.sqrt(cell_total)

    def block_step(totals, block_item):
        grad_in, grad_out = totals
        feat_block, goal_block, mask_block = block_item
        pre_act = jnp.dot(w_in.T, feat_block, preferred_element_type=jnp.float32)
        activated = jax.nn.silu(pre_act).astype(jnp.bfloat16)
        predicted = jnp.dot(w_out.T, activated, preferred_element_type=jnp.float32)
        misfit = mask_block[None, :] * (predicted - goal_block)
        act_grad = jnp.dot(w_out_wide, misfit, precision=lax.Precision.HIGHEST)
        gate_value = jax.nn.sigmoid(pre_act)
        pre_grad = (act_grad * gate_value * (1.0 + pre_act * (1.0 - gate_value))).astype(jnp.bfloat16)
        feat_grad = jnp.dot(w_in, pre_grad, preferred_element_type=jnp.float32).astype(jnp.bfloat16)
        grad_in = grad_in + jnp.dot(feat_block, pre_grad.T, preferred_element_type=jnp.float32)
        grad_out = grad_out + jnp.dot(activated.astype(jnp.float32), misfit.T, precision=lax.Precision.HIGHEST)
        return ((grad_in, grad_out), feat_grad)

    def member_step(member_item):
        member_state, goal_flux = member_item
        pieces = jnp.einsum('aci,akij->akcj', member_state.astype(jnp.float32), tiles_wide).astype(jnp.bfloat16)
        features = jnp.zeros((O_BLOCKS, C, BLK), jnp.float32)
        features = features.at[owner_block].add(pieces.reshape(-1, C, BLK).astype(jnp.float32)).astype(jnp.bfloat16)
        zeros_in = jnp.zeros((C, HID), jnp.float32)
        zeros_out = jnp.zeros((HID, Q), jnp.float32)
        (grad_in, grad_out), feat_grad = lax.scan(block_step, (zeros_in, zeros_out), (features, goal_flux, wet_cells))
        pair_grad = feat_grad[owner_block].reshape(A_BLOCKS, TOP, C, BLK).astype(jnp.float32)
        adjoint = jnp.einsum('akcj,akij->aci', pair_grad, tiles_wide)
        return (adjoint, grad_in, grad_out)
    adjoint, grad_in, grad_out = lax.map(member_step, (atm_state, target))
    return (adjoint, scale_in * lax.optimization_barrier(jnp.sum(grad_in, axis=0)), scale_out * lax.optimization_barrier(jnp.sum(grad_out, axis=0)))
```

```python
import math

import jax
import jax.numpy as jnp
from jax import lax
from jax.experimental import pallas as pl
from jax.experimental.pallas import tpu as pltpu
from jax.sharding import PartitionSpec as P


def remap_pieces(source, remap_tiles, slot_index, slot_total):
    pieces = jnp.einsum(
        "aci,akij->akcj", source, remap_tiles, preferred_element_type=jnp.float32
    ).astype(jnp.bfloat16)
    pair_count = pieces.shape[0] * pieces.shape[1]
    pieces = pieces.reshape(pair_count, source.shape[1], source.shape[2])
    return (
        jnp.zeros((slot_total, source.shape[1], source.shape[2]), jnp.bfloat16)
        .at[slot_index]
        .set(pieces)
    )


def add_pieces(received, received_ids, ocean_blocks):
    flat_data = received.reshape(-1, received.shape[2], received.shape[3]).astype(jnp.float32)
    summed = jnp.zeros((ocean_blocks + 1, received.shape[2], received.shape[3]), jnp.float32)
    summed = summed.at[received_ids.reshape(-1)].add(flat_data)
    return summed[:ocean_blocks].astype(jnp.bfloat16)


def general_body(atm_state, remap_tiles, dest_device, dest_block, wet_mask, target, w_in, w_out):
    space_size = lax.axis_size("space")
    member_size = lax.axis_size("member")
    level_size = lax.axis_size("level")
    atm_blocks, top_count, cells, _ = remap_tiles.shape
    ocean_blocks = wet_mask.shape[0]
    channels = atm_state.shape[2]
    half_chan = channels // level_size
    capacity = min(atm_blocks, max(2, 2 * atm_blocks * top_count // space_size))
    pair_count = atm_blocks * top_count
    slot_total = space_size * capacity
    dest_flat = dest_device.reshape(pair_count)
    onehot = (dest_flat[:, None] == jnp.arange(space_size, dtype=jnp.int32)[None, :]).astype(
        jnp.int32
    )
    slot_rank = jnp.sum((jnp.cumsum(onehot, axis=0) - onehot) * onehot, axis=1)
    slot_index = dest_flat * capacity + slot_rank
    send_ids = (
        jnp.full((slot_total,), ocean_blocks, jnp.int32)
        .at[slot_index]
        .set(dest_block.reshape(pair_count))
    )
    send_ids = send_ids.reshape(space_size, capacity)
    local_state = atm_state[0]
    outgoing = remap_pieces(local_state, remap_tiles, slot_index, slot_total).reshape(
        space_size, capacity, channels, cells
    )
    received, received_ids = (
        lax.all_to_all(outgoing, "space", split_axis=0, concat_axis=0, tiled=True),
        lax.all_to_all(send_ids, "space", split_axis=0, concat_axis=0, tiled=True),
    )
    features = add_pieces(received, received_ids, ocean_blocks)
    pre_act = jnp.einsum("ch,ocj->ohj", w_in, features, preferred_element_type=jnp.float32)
    activated = jax.nn.silu(pre_act).astype(jnp.bfloat16)
    partial_flux = jnp.einsum("hq,ohj->oqj", w_out, activated, preferred_element_type=jnp.float32)
    predicted = lax.psum(partial_flux, "level")
    misfit = wet_mask.astype(jnp.float32)[:, None, :] * (predicted - target[0])
    act_grad = jnp.einsum(
        "hq,oqj->ohj", w_out.astype(jnp.float32), misfit, precision=lax.Precision.HIGHEST
    )
    gate_value = jax.nn.sigmoid(pre_act)
    pre_grad = (act_grad * gate_value * (1.0 + pre_act * (1.0 - gate_value))).astype(jnp.bfloat16)
    feat_grad = lax.psum_scatter(
        jnp.einsum("ch,ohj->coj", w_in, pre_grad, preferred_element_type=jnp.float32),
        "level",
        scatter_dimension=0,
        tiled=True,
    ).astype(jnp.bfloat16)
    reply = jnp.take(feat_grad, received_ids.reshape(-1), axis=1, mode="clip")
    reply = reply.reshape(half_chan, space_size, capacity, cells)
    returned = lax.all_to_all(reply, "space", split_axis=1, concat_axis=1, tiled=True)
    pair_grad = jnp.take(returned.reshape(half_chan, slot_total, cells), slot_index, axis=1)
    pair_grad = pair_grad.reshape(half_chan, atm_blocks, top_count, cells)
    adjoint = jnp.einsum(
        "cakj,akij->aci", pair_grad, remap_tiles, preferred_element_type=jnp.float32
    )
    cell_total = member_size * space_size * ocean_blocks * cells
    scale_in = math.sqrt(w_in.shape[1] * level_size / cell_total)
    scale_out = 1.0 / math.sqrt(cell_total)
    grad_in = scale_in * jnp.einsum(
        "ocj,ohj->ch", features, pre_grad, preferred_element_type=jnp.float32
    )
    grad_out = scale_out * jnp.einsum(
        "ohj,oqj->hq",
        activated,
        misfit,
        preferred_element_type=jnp.float32,
        precision=lax.Precision.HIGHEST,
    )
    grad_in, grad_out = lax.psum((grad_in, grad_out), ("space", "member"))
    return (adjoint[None], grad_in, grad_out)


VMEM_BYTES = 48 * 1024 * 1024


def pieces_kernel(slot_ref, state_ref, tiles_ref, out_ref):
    step = pl.program_id(0)
    blocks, top_count = tiles_ref.shape[:2]
    for a in range(blocks):
        for k in range(top_count):
            slot = slot_ref[(step * blocks + a) * top_count + k]
            out_ref[slot] = jnp.dot(
                state_ref[a], tiles_ref[a, k], preferred_element_type=jnp.float32
            ).astype(jnp.bfloat16)


def slotted_pieces(slot_index, state, tiles, slot_total):
    atm_blocks, top_count, cells, _ = tiles.shape
    channels = state.shape[1]
    per_step = math.gcd(atm_blocks, 4)
    return pl.pallas_call(
        pieces_kernel,
        out_shape=jax.ShapeDtypeStruct((slot_total, channels, cells), jnp.bfloat16),
        grid_spec=pltpu.PrefetchScalarGridSpec(
            num_scalar_prefetch=1,
            grid=(atm_blocks // per_step,),
            in_specs=[
                pl.BlockSpec((per_step, channels, cells), lambda s, _: (s, 0, 0)),
                pl.BlockSpec((per_step, top_count, cells, cells), lambda s, _: (s, 0, 0, 0)),
            ],
            out_specs=pl.BlockSpec((slot_total, channels, cells), lambda s, _: (0, 0, 0)),
        ),
        compiler_params=pltpu.CompilerParams(vmem_limit_bytes=VMEM_BYTES),
    )(slot_index, state, tiles)


def adjoint_kernel(slot_ref, back_ref, tiles_ref, out_ref):
    step = pl.program_id(0)
    blocks, top_count = tiles_ref.shape[:2]
    for a in range(blocks):
        first = (step * blocks + a) * top_count
        grads = jnp.concatenate([back_ref[slot_ref[first + k]] for k in range(top_count)], axis=1)
        wide = jnp.concatenate([tiles_ref[a, k] for k in range(top_count)], axis=1)
        out_ref[a] = lax.dot_general(
            grads, wide, (((1,), (1,)), ((), ())), preferred_element_type=jnp.float32
        )


def adjoint_of(slot_index, returned, tiles):
    atm_blocks, top_count, cells, _ = tiles.shape
    slots, channels, _ = returned.shape
    per_step = math.gcd(atm_blocks, 4)
    return pl.pallas_call(
        adjoint_kernel,
        out_shape=jax.ShapeDtypeStruct((atm_blocks, channels, cells), jnp.float32),
        grid_spec=pltpu.PrefetchScalarGridSpec(
            num_scalar_prefetch=1,
            grid=(atm_blocks // per_step,),
            in_specs=[
                pl.BlockSpec((slots, channels, cells), lambda s, _: (0, 0, 0)),
                pl.BlockSpec((per_step, top_count, cells, cells), lambda s, _: (s, 0, 0, 0)),
            ],
            out_specs=pl.BlockSpec((per_step, channels, cells), lambda s, _: (s, 0, 0)),
        ),
        compiler_params=pltpu.CompilerParams(vmem_limit_bytes=VMEM_BYTES),
    )(slot_index, returned, tiles)


def network_kernel(
    scale_in,
    scale_out,
    id_ref,
    received_ref,
    mask_ref,
    goal_ref,
    w_in_ref,
    w_in_t_ref,
    w_out_t_ref,
    w_out_3_ref,
    reply_ref,
    grads_ref,
    total_ref,
    grad_ref,
    pre_ref,
    act_ref,
    out_ref,
):
    slots = received_ref.shape[0]
    ocean_blocks = goal_ref.shape[0]
    hidden, channels = w_in_t_ref.shape
    cells = received_ref.shape[2]
    group = math.gcd(ocean_blocks, 4)
    chunk = math.gcd(hidden, 256)
    total_ref[...] = jnp.zeros_like(total_ref)
    grads_ref[...] = jnp.zeros_like(grads_ref)
    out_ref[...] = jnp.zeros_like(out_ref)

    @pl.loop(0, slots)
    def _(slot):
        block = id_ref[slot]
        total_ref[block] += received_ref[slot].astype(jnp.float32)

    @pl.loop(0, ocean_blocks // group)
    def _(step):
        first = step * group
        feat = jnp.concatenate(
            [total_ref[first + g].astype(jnp.bfloat16) for g in range(group)], axis=1
        )
        predicted = jnp.zeros((8, group * cells), jnp.float32)
        for h in range(0, hidden, chunk):
            rows = slice(h, h + chunk)
            pre = jnp.dot(w_in_t_ref[rows], feat, preferred_element_type=jnp.float32)
            pre_ref[rows] = pre
            act = (pre * jax.nn.sigmoid(pre)).astype(jnp.bfloat16)
            act_ref[rows] = act
            predicted += jnp.dot(w_out_t_ref[:, rows], act, preferred_element_type=jnp.float32)
        goal = jnp.concatenate([goal_ref[first + g] for g in range(group)], axis=1)
        mask = jnp.concatenate([mask_ref[first + g] for g in range(group)], axis=1)
        misfit = mask * (predicted - goal)
        high = misfit.astype(jnp.bfloat16).astype(jnp.float32)
        rest = misfit - high
        middle = rest.astype(jnp.bfloat16).astype(jnp.float32)
        low = rest - middle
        misfit_3 = jnp.concatenate([high, middle, low, jnp.zeros_like(low)], axis=0).astype(
            jnp.bfloat16
        )
        feat_grad = jnp.zeros((channels, group * cells), jnp.float32)
        for h in range(0, hidden, chunk):
            rows = slice(h, h + chunk)
            act_grad = jnp.dot(w_out_3_ref[rows], misfit_3, preferred_element_type=jnp.float32)
            pre = pre_ref[rows]
            gate = jax.nn.sigmoid(pre)
            pre_grad = (act_grad * gate * (1.0 + pre * (1.0 - gate))).astype(jnp.bfloat16)
            feat_grad += jnp.dot(w_in_ref[:, rows], pre_grad, preferred_element_type=jnp.float32)
            grads_ref[0:channels, rows] += lax.dot_general(
                feat, pre_grad, (((1,), (1,)), ((), ())), preferred_element_type=jnp.float32
            )
            out_ref[:, rows] += lax.dot_general(
                misfit_3, act_ref[rows], (((1,), (1,)), ((), ())), preferred_element_type=jnp.float32
            )
        for g in range(group):
            grad_ref[first + g] = feat_grad[:, g * cells : (g + 1) * cells].astype(jnp.bfloat16)

    grads_ref[0:channels] = scale_in * grads_ref[0:channels]
    grads_ref[channels : channels + 8] = scale_out * (out_ref[0:8] + out_ref[8:16] + out_ref[16:24])

    @pl.loop(0, slots)
    def _(slot):
        reply_ref[slot] = grad_ref[jnp.minimum(id_ref[slot], ocean_blocks - 1)]


def network(received, ids, wet_mask, target, w_in, w_out, scale_in, scale_out):
    slots, channels, cells = received.shape
    ocean_blocks, outputs, _ = target.shape
    hidden = w_in.shape[1]
    group = math.gcd(ocean_blocks, 4)
    padded = jnp.pad(w_out, ((0, 0), (0, 8 - outputs)))
    whole = pl.BlockSpec(memory_space=pltpu.VMEM)
    return pl.pallas_call(
        lambda *refs: network_kernel(scale_in, scale_out, *refs),
        out_shape=(
            jax.ShapeDtypeStruct((slots, channels, cells), jnp.bfloat16),
            jax.ShapeDtypeStruct((channels + 8, hidden), jnp.float32),
        ),
        in_specs=[pl.BlockSpec(memory_space=pltpu.SMEM)] + [whole] * 7,
        out_specs=(whole, whole),
        scratch_shapes=[
            pltpu.VMEM((ocean_blocks + 1, channels, cells), jnp.float32),
            pltpu.VMEM((ocean_blocks, channels, cells), jnp.bfloat16),
            pltpu.VMEM((hidden, group * cells), jnp.float32),
            pltpu.VMEM((hidden, group * cells), jnp.bfloat16),
            pltpu.VMEM((32, hidden), jnp.float32),
        ],
        compiler_params=pltpu.CompilerParams(vmem_limit_bytes=VMEM_BYTES),
    )(
        ids,
        received,
        wet_mask.astype(jnp.float32)[:, None, :],
        jnp.pad(target, ((0, 0), (0, 8 - outputs), (0, 0))),
        w_in,
        w_in.T,
        padded.T,
        jnp.concatenate([padded, padded, padded, jnp.zeros_like(padded)], axis=1),
    )


def fused_body(atm_state, remap_tiles, dest_device, dest_block, wet_mask, target, w_in, w_out):
    space_size = lax.axis_size("space")
    member_size = lax.axis_size("member")
    atm_blocks, top_count, cells, _ = remap_tiles.shape
    ocean_blocks = wet_mask.shape[0]
    channels = atm_state.shape[2]
    capacity = min(atm_blocks, max(2, 2 * atm_blocks * top_count // space_size))
    pair_count = atm_blocks * top_count
    slot_total = space_size * capacity
    dest_flat = dest_device.reshape(pair_count)
    onehot = (dest_flat[:, None] == jnp.arange(space_size, dtype=jnp.int32)[None, :]).astype(
        jnp.int32
    )
    slot_rank = jnp.sum((jnp.cumsum(onehot, axis=0) - onehot) * onehot, axis=1)
    slot_index = dest_flat * capacity + slot_rank
    send_ids = (
        jnp.full((slot_total,), ocean_blocks, jnp.int32)
        .at[slot_index]
        .set(dest_block.reshape(pair_count))
    )
    received_ids = lax.all_to_all(
        send_ids.reshape(space_size, capacity), "space", split_axis=0, concat_axis=0, tiled=True
    ).reshape(slot_total)
    outgoing = slotted_pieces(slot_index, atm_state[0], remap_tiles, slot_total)
    received = lax.all_to_all(
        outgoing.reshape(space_size, capacity, channels, cells),
        "space",
        split_axis=0,
        concat_axis=0,
        tiled=True,
    ).reshape(slot_total, channels, cells)
    cell_total = member_size * space_size * ocean_blocks * cells
    scale_in = math.sqrt(w_in.shape[1] / cell_total)
    scale_out = 1.0 / math.sqrt(cell_total)
    reply, grads = network(
        received, received_ids, wet_mask, target[0], w_in, w_out, scale_in, scale_out
    )
    returned = lax.all_to_all(
        reply.reshape(space_size, capacity, channels, cells),
        "space",
        split_axis=0,
        concat_axis=0,
        tiled=True,
    ).reshape(slot_total, channels, cells)
    grads = lax.psum(grads, ("space", "member"))
    adjoint = adjoint_of(slot_index, returned, remap_tiles)
    return (adjoint[None], grads[:channels], grads[channels : channels + w_out.shape[1]].T)


def solution(mesh):
    body = fused_body if mesh.shape["level"] == 1 else general_body
    return jax.shard_map(
        body,
        mesh=mesh,
        in_specs=(
            P("member", ("group", "space"), None, None),
            P("space", None, None, None),
            P("space", None),
            P("space", None),
            P("space", None),
            P("member", ("group", "space"), None, None),
            P(None, "level"),
            P("level", None),
        ),
        out_specs=(
            P("member", ("group", "space"), "level", None),
            P("group", "level"),
            P("level", "group"),
        ),
        check_vma=False,
    )
```

```python
import math

import jax
import jax.numpy as jnp
from jax import lax
from jax.experimental import pallas as pl
from jax.experimental.pallas import tpu as pltpu
from jax.sharding import PartitionSpec as P


def remap_pieces(source, remap_tiles, slot_index, slot_total):
    pieces = jnp.einsum(
        "aci,akij->akcj", source, remap_tiles, preferred_element_type=jnp.float32
    ).astype(jnp.bfloat16)
    pair_count = pieces.shape[0] * pieces.shape[1]
    pieces = pieces.reshape(pair_count, source.shape[1], source.shape[2])
    return (
        jnp.zeros((slot_total, source.shape[1], source.shape[2]), jnp.bfloat16)
        .at[slot_index]
        .set(pieces)
    )


def add_pieces(received, received_ids, ocean_blocks):
    flat_data = received.reshape(-1, received.shape[2], received.shape[3]).astype(jnp.float32)
    summed = jnp.zeros((ocean_blocks + 1, received.shape[2], received.shape[3]), jnp.float32)
    summed = summed.at[received_ids.reshape(-1)].add(flat_data)
    return summed[:ocean_blocks].astype(jnp.bfloat16)


def general_body(atm_state, remap_tiles, dest_device, dest_block, wet_mask, target, w_in, w_out):
    space_size = lax.axis_size("space")
    member_size = lax.axis_size("member")
    level_size = lax.axis_size("level")
    atm_blocks, top_count, cells, _ = remap_tiles.shape
    ocean_blocks = wet_mask.shape[0]
    channels = atm_state.shape[2]
    half_chan = channels // level_size
    capacity = min(atm_blocks, max(2, 2 * atm_blocks * top_count // space_size))
    pair_count = atm_blocks * top_count
    slot_total = space_size * capacity
    dest_flat = dest_device.reshape(pair_count)
    onehot = (dest_flat[:, None] == jnp.arange(space_size, dtype=jnp.int32)[None, :]).astype(
        jnp.int32
    )
    slot_rank = jnp.sum((jnp.cumsum(onehot, axis=0) - onehot) * onehot, axis=1)
    slot_index = dest_flat * capacity + slot_rank
    send_ids = (
        jnp.full((slot_total,), ocean_blocks, jnp.int32)
        .at[slot_index]
        .set(dest_block.reshape(pair_count))
    )
    send_ids = send_ids.reshape(space_size, capacity)
    local_state = atm_state[0]
    outgoing = remap_pieces(local_state, remap_tiles, slot_index, slot_total).reshape(
        space_size, capacity, channels, cells
    )
    received, received_ids = (
        lax.all_to_all(outgoing, "space", split_axis=0, concat_axis=0, tiled=True),
        lax.all_to_all(send_ids, "space", split_axis=0, concat_axis=0, tiled=True),
    )
    features = add_pieces(received, received_ids, ocean_blocks)
    pre_act = jnp.einsum("ch,ocj->ohj", w_in, features, preferred_element_type=jnp.float32)
    activated = jax.nn.silu(pre_act).astype(jnp.bfloat16)
    partial_flux = jnp.einsum("hq,ohj->oqj", w_out, activated, preferred_element_type=jnp.float32)
    predicted = lax.psum(partial_flux, "level")
    misfit = wet_mask.astype(jnp.float32)[:, None, :] * (predicted - target[0])
    act_grad = jnp.einsum(
        "hq,oqj->ohj", w_out.astype(jnp.float32), misfit, precision=lax.Precision.HIGHEST
    )
    gate_value = jax.nn.sigmoid(pre_act)
    pre_grad = (act_grad * gate_value * (1.0 + pre_act * (1.0 - gate_value))).astype(jnp.bfloat16)
    feat_grad = lax.psum_scatter(
        jnp.einsum("ch,ohj->coj", w_in, pre_grad, preferred_element_type=jnp.float32),
        "level",
        scatter_dimension=0,
        tiled=True,
    ).astype(jnp.bfloat16)
    reply = jnp.take(feat_grad, received_ids.reshape(-1), axis=1, mode="clip")
    reply = reply.reshape(half_chan, space_size, capacity, cells)
    returned = lax.all_to_all(reply, "space", split_axis=1, concat_axis=1, tiled=True)
    pair_grad = jnp.take(returned.reshape(half_chan, slot_total, cells), slot_index, axis=1)
    pair_grad = pair_grad.reshape(half_chan, atm_blocks, top_count, cells)
    adjoint = jnp.einsum(
        "cakj,akij->aci", pair_grad, remap_tiles, preferred_element_type=jnp.float32
    )
    cell_total = member_size * space_size * ocean_blocks * cells
    scale_in = math.sqrt(w_in.shape[1] * level_size / cell_total)
    scale_out = 1.0 / math.sqrt(cell_total)
    grad_in = scale_in * jnp.einsum(
        "ocj,ohj->ch", features, pre_grad, preferred_element_type=jnp.float32
    )
    grad_out = scale_out * jnp.einsum(
        "ohj,oqj->hq",
        activated,
        misfit,
        preferred_element_type=jnp.float32,
        precision=lax.Precision.HIGHEST,
    )
    grad_in, grad_out = lax.psum((grad_in, grad_out), ("space", "member"))
    return (adjoint[None], grad_in, grad_out)


VMEM_BYTES = 48 * 1024 * 1024


def pieces_kernel(slot_ref, state_ref, tiles_ref, out_ref):
    step = pl.program_id(0)
    blocks, top_count = tiles_ref.shape[:2]
    for a in range(blocks):
        for k in range(top_count):
            slot = slot_ref[(step * blocks + a) * top_count + k]
            out_ref[slot] = jnp.dot(
                state_ref[a], tiles_ref[a, k], preferred_element_type=jnp.float32
            ).astype(jnp.bfloat16)


def slotted_pieces(slot_index, state, tiles, slot_total):
    atm_blocks, top_count, cells, _ = tiles.shape
    channels = state.shape[1]
    per_step = math.gcd(atm_blocks, 4)
    return pl.pallas_call(
        pieces_kernel,
        out_shape=jax.ShapeDtypeStruct((slot_total, channels, cells), jnp.bfloat16),
        grid_spec=pltpu.PrefetchScalarGridSpec(
            num_scalar_prefetch=1,
            grid=(atm_blocks // per_step,),
            in_specs=[
                pl.BlockSpec((per_step, channels, cells), lambda s, _: (s, 0, 0)),
                pl.BlockSpec((per_step, top_count, cells, cells), lambda s, _: (s, 0, 0, 0)),
            ],
            out_specs=pl.BlockSpec((slot_total, channels, cells), lambda s, _: (0, 0, 0)),
        ),
        compiler_params=pltpu.CompilerParams(vmem_limit_bytes=VMEM_BYTES),
    )(slot_index, state, tiles)


def adjoint_kernel(slot_ref, back_ref, tiles_ref, out_ref):
    step = pl.program_id(0)
    blocks, top_count = tiles_ref.shape[:2]
    for a in range(blocks):
        first = (step * blocks + a) * top_count
        grads = jnp.concatenate([back_ref[slot_ref[first + k]] for k in range(top_count)], axis=1)
        wide = jnp.concatenate([tiles_ref[a, k] for k in range(top_count)], axis=1)
        out_ref[a] = lax.dot_general(
            grads, wide, (((1,), (1,)), ((), ())), preferred_element_type=jnp.float32
        )


def adjoint_of(slot_index, returned, tiles):
    atm_blocks, top_count, cells, _ = tiles.shape
    slots, channels, _ = returned.shape
    per_step = math.gcd(atm_blocks, 4)
    return pl.pallas_call(
        adjoint_kernel,
        out_shape=jax.ShapeDtypeStruct((atm_blocks, channels, cells), jnp.float32),
        grid_spec=pltpu.PrefetchScalarGridSpec(
            num_scalar_prefetch=1,
            grid=(atm_blocks // per_step,),
            in_specs=[
                pl.BlockSpec((slots, channels, cells), lambda s, _: (0, 0, 0)),
                pl.BlockSpec((per_step, top_count, cells, cells), lambda s, _: (s, 0, 0, 0)),
            ],
            out_specs=pl.BlockSpec((per_step, channels, cells), lambda s, _: (s, 0, 0)),
        ),
        compiler_params=pltpu.CompilerParams(vmem_limit_bytes=VMEM_BYTES),
    )(slot_index, returned, tiles)


def network_kernel(
    scale_in,
    scale_out,
    id_ref,
    received_ref,
    mask_ref,
    goal_ref,
    w_in_ref,
    w_in_t_ref,
    w_out_t_ref,
    w_out_3_ref,
    grad_ref,
    pieces_ref,
    total_ref,
    grads_ref,
    pre_ref,
    act_ref,
    out_ref,
):
    slots = received_ref.shape[0]
    ocean_blocks = goal_ref.shape[0]
    hidden, channels = w_in_t_ref.shape
    cells = received_ref.shape[2]
    group = math.gcd(ocean_blocks, 4)
    chunk = math.gcd(hidden, 256)
    total_ref[...] = jnp.zeros_like(total_ref)
    grads_ref[...] = jnp.zeros_like(grads_ref)
    out_ref[...] = jnp.zeros_like(out_ref)

    @pl.loop(0, slots)
    def _(slot):
        block = id_ref[slot]
        total_ref[block] += received_ref[slot].astype(jnp.float32)

    @pl.loop(0, ocean_blocks // group)
    def _(step):
        first = step * group
        feat = jnp.concatenate(
            [total_ref[first + g].astype(jnp.bfloat16) for g in range(group)], axis=1
        )
        predicted = jnp.zeros((8, group * cells), jnp.float32)
        for h in range(0, hidden, chunk):
            rows = slice(h, h + chunk)
            pre = jnp.dot(w_in_t_ref[rows], feat, preferred_element_type=jnp.float32)
            pre_ref[rows] = pre
            act = (pre * jax.nn.sigmoid(pre)).astype(jnp.bfloat16)
            act_ref[rows] = act
            predicted += jnp.dot(w_out_t_ref[:, rows], act, preferred_element_type=jnp.float32)
        goal = jnp.concatenate([goal_ref[first + g] for g in range(group)], axis=1)
        mask = jnp.concatenate([mask_ref[first + g] for g in range(group)], axis=1)
        misfit = mask * (predicted - goal)
        high = misfit.astype(jnp.bfloat16).astype(jnp.float32)
        rest = misfit - high
        middle = rest.astype(jnp.bfloat16).astype(jnp.float32)
        low = rest - middle
        misfit_3 = jnp.concatenate([high, middle, low, jnp.zeros_like(low)], axis=0).astype(
            jnp.bfloat16
        )
        feat_grad = jnp.zeros((channels, group * cells), jnp.float32)
        for h in range(0, hidden, chunk):
            rows = slice(h, h + chunk)
            act_grad = jnp.dot(w_out_3_ref[rows], misfit_3, preferred_element_type=jnp.float32)
            pre = pre_ref[rows]
            gate = jax.nn.sigmoid(pre)
            pre_grad = (act_grad * gate * (1.0 + pre * (1.0 - gate))).astype(jnp.bfloat16)
            feat_grad += jnp.dot(w_in_ref[:, rows], pre_grad, preferred_element_type=jnp.float32)
            grads_ref[:, rows] += lax.dot_general(
                feat, pre_grad, (((1,), (1,)), ((), ())), preferred_element_type=jnp.float32
            )
            out_ref[:, rows] += lax.dot_general(
                misfit_3, act_ref[rows], (((1,), (1,)), ((), ())), preferred_element_type=jnp.float32
            )
        for g in range(group):
            grad_ref[first + g] = feat_grad[:, g * cells : (g + 1) * cells].astype(jnp.bfloat16)

    out = scale_out * (out_ref[0:8] + out_ref[8:16] + out_ref[16:24])
    for p in range(pieces_ref.shape[0]):
        pieces_ref[p, :, 0:hidden] = scale_in * grads_ref[8 * p : 8 * p + 8]
        if (p + 1) * 128 <= hidden:
            pieces_ref[p, :, hidden : hidden + 128] = out[:, p * 128 : (p + 1) * 128]
        else:
            pieces_ref[p, :, hidden : hidden + 128] = jnp.zeros((8, 128), jnp.float32)


def network(received, ids, wet_mask, target, w_in, w_out, scale_in, scale_out):
    slots, channels, cells = received.shape
    ocean_blocks, outputs, _ = target.shape
    hidden = w_in.shape[1]
    group = math.gcd(ocean_blocks, 4)
    padded = jnp.pad(w_out, ((0, 0), (0, 8 - outputs)))
    whole = pl.BlockSpec(memory_space=pltpu.VMEM)
    return pl.pallas_call(
        lambda *refs: network_kernel(scale_in, scale_out, *refs),
        out_shape=(
            jax.ShapeDtypeStruct((ocean_blocks, channels, cells), jnp.bfloat16),
            jax.ShapeDtypeStruct((channels // 8, 8, hidden + 128), jnp.float32),
        ),
        in_specs=[pl.BlockSpec(memory_space=pltpu.SMEM)] + [whole] * 7,
        out_specs=(whole, whole),
        scratch_shapes=[
            pltpu.VMEM((ocean_blocks + 1, channels, cells), jnp.float32),
            pltpu.VMEM((channels, hidden), jnp.float32),
            pltpu.VMEM((hidden, group * cells), jnp.float32),
            pltpu.VMEM((hidden, group * cells), jnp.bfloat16),
            pltpu.VMEM((32, hidden), jnp.float32),
        ],
        compiler_params=pltpu.CompilerParams(vmem_limit_bytes=VMEM_BYTES),
    )(
        ids,
        received,
        wet_mask.astype(jnp.float32)[:, None, :],
        jnp.pad(target, ((0, 0), (0, 8 - outputs), (0, 0))),
        w_in,
        w_in.T,
        padded.T,
        jnp.concatenate([padded, padded, padded, jnp.zeros_like(padded)], axis=1),
    )


CHUNKS = 2
MESH = pl.DeviceIdType.MESH


def exchange_kernel(
    space_size,
    member_size,
    feat_ref,
    grads_ref,
    all_ref,
    sums_ref,
    inbox,
    total,
    term_send,
    term_recv,
    sum_send,
    sum_recv,
    line_send,
    line_recv,
    pair_send,
    pair_recv,
    own_sem,
):
    space, member = lax.axis_index("space"), lax.axis_index("member")
    ranks = space_size * member_size
    rank = member * space_size + space
    length = space_size // 2
    place, core = space // 2, space % 2
    size = feat_ref.shape[0] // CHUNKS

    def peer(i):
        other = lax.rem(rank + i, ranks)
        return other, {"space": other % space_size, "member": other // space_size}

    barrier = pltpu.get_barrier_semaphore()
    for i in range(1, ranks):
        pl.semaphore_signal(barrier, inc=1, device_id=peer(i)[1], device_id_type=MESH)
    pl.semaphore_wait(barrier, ranks - 1)

    def term(i):
        other, device = peer(i)
        return pltpu.make_async_remote_copy(
            src_ref=grads_ref.at[other],
            dst_ref=inbox.at[i - 1],
            send_sem=term_send.at[i - 1],
            recv_sem=term_recv.at[i - 1],
            device_id=device,
            device_id_type=MESH,
        )

    def piece(i, owner):
        return pltpu.make_async_remote_copy(
            src_ref=total,
            dst_ref=sums_ref.at[owner],
            send_sem=sum_send.at[i - 1],
            recv_sem=sum_recv.at[i - 1],
            device_id=peer(i)[1],
            device_id_type=MESH,
        )

    def source(origin, own, c):
        rows = pl.ds(c * size, size)
        return feat_ref.at[rows] if own else all_ref.at[origin, rows]

    def line(way, hop, c, origin, own):
        step = 1 if way == 0 else -1
        return pltpu.make_async_remote_copy(
            src_ref=source(origin, own, c),
            dst_ref=all_ref.at[origin, pl.ds(c * size, size)],
            send_sem=line_send.at[way, hop, c],
            recv_sem=line_recv.at[way, hop, c],
            device_id={"space": (place + step) * 2 + core},
            device_id_type=MESH,
        )

    def pair(index, c, origin, own):
        return pltpu.make_async_remote_copy(
            src_ref=source(origin, own, c),
            dst_ref=all_ref.at[origin, pl.ds(c * size, size)],
            send_sem=pair_send.at[index, c],
            recv_sem=pair_recv.at[index, c],
            device_id={"space": place * 2 + 1 - core},
            device_id_type=MESH,
        )

    def behind(way, hop):
        at = place - 1 - hop if way == 0 else place + 1 + hop
        return at, (at >= 0 if way == 0 else at < length)

    ahead = (place < length - 1, place > 0)
    own_copy = pltpu.make_async_copy(feat_ref, all_ref.at[space], own_sem.at[0])
    for c in range(CHUNKS):
        for way in range(2):

            @pl.when(ahead[way])
            def _():
                line(way, 0, c, space, True).start()

    for i in range(1, ranks):
        term(i).start()
    for c in range(CHUNKS):
        pair(0, c, space, True).start()
    own_copy.start()

    for hop in range(length - 1):
        for c in range(CHUNKS):
            for way in range(2):
                at, there = behind(way, hop)
                origin = at * 2 + core

                @pl.when(there)
                def _():
                    line(way, hop, c, origin, False).wait_recv()
                    if hop + 1 < length - 1:

                        @pl.when(ahead[way])
                        def _():
                            line(way, hop + 1, c, origin, False).start()

                    pair(1 + way * (length - 1) + hop, c, origin, False).start()

        if hop == 0:
            for i in range(1, ranks):
                term(i).wait_recv()
            value = grads_ref[rank]
            for i in range(1, ranks):
                value += inbox[i - 1]
            total[...] = value
            for i in range(1, ranks):
                piece(i, rank).start()
            own_sum = pltpu.make_async_copy(total, sums_ref.at[rank], own_sem.at[1])
            own_sum.start()

    own_copy.wait()
    own_sum.wait()
    for i in range(1, ranks):
        piece(i, lax.rem(rank + ranks - i, ranks)).wait_recv()
        piece(i, rank).wait_send()
        term(i).wait_send()
    for c in range(CHUNKS):
        pair(0, c, space, True).wait_send()
        pair(0, c, place * 2 + 1 - core, False).wait_recv()
        for way in range(2):

            @pl.when(ahead[way])
            def _():
                line(way, 0, c, space, True).wait_send()

            for hop in range(length - 1):
                at, there = behind(way, hop)
                origin = at * 2 + core
                index = 1 + way * (length - 1) + hop

                @pl.when(there)
                def _():
                    if hop + 1 < length - 1:

                        @pl.when(ahead[way])
                        def _():
                            line(way, hop + 1, c, origin, False).wait_send()

                    pair(index, c, origin, False).wait_send()
                    pair(index, c, at * 2 + 1 - core, False).wait_recv()


def exchange(feat_grad, grads, space_size, member_size):
    peers = space_size * member_size - 1
    hops = max(1, space_size // 2 - 1)
    dma = pltpu.SemaphoreType.DMA
    anywhere = pl.BlockSpec(memory_space=pl.ANY)
    return pl.pallas_call(
        lambda *refs: exchange_kernel(space_size, member_size, *refs),
        out_shape=(
            jax.ShapeDtypeStruct((space_size,) + feat_grad.shape, feat_grad.dtype),
            jax.ShapeDtypeStruct(grads.shape, grads.dtype),
        ),
        in_specs=[anywhere, pl.BlockSpec(memory_space=pltpu.VMEM)],
        out_specs=(anywhere, anywhere),
        scratch_shapes=[
            pltpu.VMEM((peers,) + grads.shape[1:], grads.dtype),
            pltpu.VMEM(grads.shape[1:], grads.dtype),
            dma((peers,)),
            dma((peers,)),
            dma((peers,)),
            dma((peers,)),
            dma((2, hops, CHUNKS)),
            dma((2, hops, CHUNKS)),
            dma((1 + 2 * hops, CHUNKS)),
            dma((1 + 2 * hops, CHUNKS)),
            dma((2,)),
        ],
        compiler_params=pltpu.CompilerParams(
            collective_id=0, has_side_effects=True, vmem_limit_bytes=VMEM_BYTES
        ),
    )(feat_grad, grads)


def fused_body(atm_state, remap_tiles, dest_device, dest_block, wet_mask, target, w_in, w_out):
    space_size = lax.axis_size("space")
    member_size = lax.axis_size("member")
    atm_blocks, top_count, cells, _ = remap_tiles.shape
    ocean_blocks = wet_mask.shape[0]
    channels = atm_state.shape[2]
    pieces_fit = channels == 8 * space_size * member_size and w_in.shape[1] <= 16 * channels
    if not pieces_fit or ocean_blocks % CHUNKS:
        return general_body(
            atm_state, remap_tiles, dest_device, dest_block, wet_mask, target, w_in, w_out
        )
    capacity = min(atm_blocks, max(2, 2 * atm_blocks * top_count // space_size))
    pair_count = atm_blocks * top_count
    slot_total = space_size * capacity
    dest_flat = dest_device.reshape(pair_count)
    onehot = (dest_flat[:, None] == jnp.arange(space_size, dtype=jnp.int32)[None, :]).astype(
        jnp.int32
    )
    slot_rank = jnp.sum((jnp.cumsum(onehot, axis=0) - onehot) * onehot, axis=1)
    slot_index = dest_flat * capacity + slot_rank
    send_ids = (
        jnp.full((slot_total,), ocean_blocks, jnp.int32)
        .at[slot_index]
        .set(dest_block.reshape(pair_count))
    )
    received_ids = lax.all_to_all(
        send_ids.reshape(space_size, capacity), "space", split_axis=0, concat_axis=0, tiled=True
    ).reshape(slot_total)
    outgoing = slotted_pieces(slot_index, atm_state[0], remap_tiles, slot_total)
    received = lax.all_to_all(
        outgoing.reshape(space_size, capacity, channels, cells),
        "space",
        split_axis=0,
        concat_axis=0,
        tiled=True,
    ).reshape(slot_total, channels, cells)
    cell_total = member_size * space_size * ocean_blocks * cells
    scale_in = math.sqrt(w_in.shape[1] / cell_total)
    scale_out = 1.0 / math.sqrt(cell_total)
    feat_grad, grads = network(
        received, received_ids, wet_mask, target[0], w_in, w_out, scale_in, scale_out
    )
    gathered, summed = exchange(feat_grad, grads, space_size, member_size)
    owner = dest_flat * ocean_blocks + dest_block.reshape(pair_count)
    adjoint = adjoint_of(
        owner, gathered.reshape(space_size * ocean_blocks, channels, cells), remap_tiles
    )
    hidden, outputs = w_out.shape
    grad_in = summed[:, :, :hidden].reshape(channels, hidden)
    grad_out = summed[: hidden // 128, :outputs, hidden:]
    return (adjoint[None], grad_in, grad_out.transpose(0, 2, 1).reshape(hidden, outputs))


def solution(mesh):
    body = fused_body if mesh.shape["level"] == 1 and mesh.shape["space"] % 2 == 0 else general_body
    return jax.shard_map(
        body,
        mesh=mesh,
        in_specs=(
            P("member", ("group", "space"), None, None),
            P("space", None, None, None),
            P("space", None),
            P("space", None),
            P("space", None),
            P("member", ("group", "space"), None, None),
            P(None, "level"),
            P("level", None),
        ),
        out_specs=(
            P("member", ("group", "space"), "level", None),
            P("group", "level"),
            P("level", "group"),
        ),
        check_vma=False,
    )
```

```python
import math

import jax
import jax.numpy as jnp
from jax import lax
from jax.experimental import pallas as pl
from jax.experimental.pallas import tpu as pltpu
from jax.sharding import PartitionSpec as P


def remap_pieces(source, remap_tiles, slot_index, slot_total):
    pieces = jnp.einsum(
        "aci,akij->akcj", source, remap_tiles, preferred_element_type=jnp.float32
    ).astype(jnp.bfloat16)
    pair_count = pieces.shape[0] * pieces.shape[1]
    pieces = pieces.reshape(pair_count, source.shape[1], source.shape[2])
    return (
        jnp.zeros((slot_total, source.shape[1], source.shape[2]), jnp.bfloat16)
        .at[slot_index]
        .set(pieces)
    )


def add_pieces(received, received_ids, ocean_blocks):
    flat_data = received.reshape(-1, received.shape[2], received.shape[3]).astype(jnp.float32)
    summed = jnp.zeros((ocean_blocks + 1, received.shape[2], received.shape[3]), jnp.float32)
    summed = summed.at[received_ids.reshape(-1)].add(flat_data)
    return summed[:ocean_blocks].astype(jnp.bfloat16)


def general_body(atm_state, remap_tiles, dest_device, dest_block, wet_mask, target, w_in, w_out):
    space_size = lax.axis_size("space")
    member_size = lax.axis_size("member")
    level_size = lax.axis_size("level")
    atm_blocks, top_count, cells, _ = remap_tiles.shape
    ocean_blocks = wet_mask.shape[0]
    channels = atm_state.shape[2]
    half_chan = channels // level_size
    capacity = min(atm_blocks, max(2, 2 * atm_blocks * top_count // space_size))
    pair_count = atm_blocks * top_count
    slot_total = space_size * capacity
    dest_flat = dest_device.reshape(pair_count)
    onehot = (dest_flat[:, None] == jnp.arange(space_size, dtype=jnp.int32)[None, :]).astype(
        jnp.int32
    )
    slot_rank = jnp.sum((jnp.cumsum(onehot, axis=0) - onehot) * onehot, axis=1)
    slot_index = dest_flat * capacity + slot_rank
    send_ids = (
        jnp.full((slot_total,), ocean_blocks, jnp.int32)
        .at[slot_index]
        .set(dest_block.reshape(pair_count))
    )
    send_ids = send_ids.reshape(space_size, capacity)
    local_state = atm_state[0]
    outgoing = remap_pieces(local_state, remap_tiles, slot_index, slot_total).reshape(
        space_size, capacity, channels, cells
    )
    received, received_ids = (
        lax.all_to_all(outgoing, "space", split_axis=0, concat_axis=0, tiled=True),
        lax.all_to_all(send_ids, "space", split_axis=0, concat_axis=0, tiled=True),
    )
    features = add_pieces(received, received_ids, ocean_blocks)
    pre_act = jnp.einsum("ch,ocj->ohj", w_in, features, preferred_element_type=jnp.float32)
    activated = jax.nn.silu(pre_act).astype(jnp.bfloat16)
    partial_flux = jnp.einsum("hq,ohj->oqj", w_out, activated, preferred_element_type=jnp.float32)
    predicted = lax.psum(partial_flux, "level")
    misfit = wet_mask.astype(jnp.float32)[:, None, :] * (predicted - target[0])
    act_grad = jnp.einsum(
        "hq,oqj->ohj", w_out.astype(jnp.float32), misfit, precision=lax.Precision.HIGHEST
    )
    gate_value = jax.nn.sigmoid(pre_act)
    pre_grad = (act_grad * gate_value * (1.0 + pre_act * (1.0 - gate_value))).astype(jnp.bfloat16)
    feat_grad = lax.psum_scatter(
        jnp.einsum("ch,ohj->coj", w_in, pre_grad, preferred_element_type=jnp.float32),
        "level",
        scatter_dimension=0,
        tiled=True,
    ).astype(jnp.bfloat16)
    reply = jnp.take(feat_grad, received_ids.reshape(-1), axis=1, mode="clip")
    reply = reply.reshape(half_chan, space_size, capacity, cells)
    returned = lax.all_to_all(reply, "space", split_axis=1, concat_axis=1, tiled=True)
    pair_grad = jnp.take(returned.reshape(half_chan, slot_total, cells), slot_index, axis=1)
    pair_grad = pair_grad.reshape(half_chan, atm_blocks, top_count, cells)
    adjoint = jnp.einsum(
        "cakj,akij->aci", pair_grad, remap_tiles, preferred_element_type=jnp.float32
    )
    cell_total = member_size * space_size * ocean_blocks * cells
    scale_in = math.sqrt(w_in.shape[1] * level_size / cell_total)
    scale_out = 1.0 / math.sqrt(cell_total)
    grad_in = scale_in * jnp.einsum(
        "ocj,ohj->ch", features, pre_grad, preferred_element_type=jnp.float32
    )
    grad_out = scale_out * jnp.einsum(
        "ohj,oqj->hq",
        activated,
        misfit,
        preferred_element_type=jnp.float32,
        precision=lax.Precision.HIGHEST,
    )
    grad_in, grad_out = lax.psum((grad_in, grad_out), ("space", "member"))
    return (adjoint[None], grad_in, grad_out)


VMEM_BYTES = 48 * 1024 * 1024


def slots_kernel(pair_ref, tiles_ref, out_ref):
    @pl.loop(0, out_ref.shape[0], unroll=4)
    def _(slot):
        out_ref[slot] = tiles_ref[pair_ref[slot]]


def slotted_tiles(pairs, tiles):
    whole = pl.BlockSpec(memory_space=pltpu.VMEM)
    return pl.pallas_call(
        slots_kernel,
        out_shape=jax.ShapeDtypeStruct(pairs.shape + tiles.shape[1:], tiles.dtype),
        in_specs=[pl.BlockSpec(memory_space=pltpu.SMEM), whole],
        out_specs=whole,
        compiler_params=pltpu.CompilerParams(vmem_limit_bytes=VMEM_BYTES),
    )(pairs, tiles)


def adjoint_kernel(slot_ref, back_ref, tiles_ref, out_ref):
    step = pl.program_id(0)
    blocks, top_count = tiles_ref.shape[:2]
    for a in range(blocks):
        first = (step * blocks + a) * top_count
        grads = jnp.concatenate([back_ref[slot_ref[first + k]] for k in range(top_count)], axis=1)
        wide = jnp.concatenate([tiles_ref[a, k] for k in range(top_count)], axis=1)
        out_ref[a] = lax.dot_general(
            grads, wide, (((1,), (1,)), ((), ())), preferred_element_type=jnp.float32
        )


def adjoint_of(slot_index, returned, tiles):
    atm_blocks, top_count, cells, _ = tiles.shape
    slots, channels, _ = returned.shape
    per_step = math.gcd(atm_blocks, 4)
    return pl.pallas_call(
        adjoint_kernel,
        out_shape=jax.ShapeDtypeStruct((atm_blocks, channels, cells), jnp.float32),
        grid_spec=pltpu.PrefetchScalarGridSpec(
            num_scalar_prefetch=1,
            grid=(atm_blocks // per_step,),
            in_specs=[
                pl.BlockSpec((slots, channels, cells), lambda s, _: (0, 0, 0)),
                pl.BlockSpec((per_step, top_count, cells, cells), lambda s, _: (s, 0, 0, 0)),
            ],
            out_specs=pl.BlockSpec((per_step, channels, cells), lambda s, _: (s, 0, 0)),
        ),
        compiler_params=pltpu.CompilerParams(vmem_limit_bytes=VMEM_BYTES),
    )(slot_index, returned, tiles)


def network_kernel(
    scale_in,
    scale_out,
    id_ref,
    state_at_ref,
    states_ref,
    slots_ref,
    mask_ref,
    goal_ref,
    w_in_ref,
    w_in_t_ref,
    w_out_t_ref,
    w_out_3_ref,
    grad_ref,
    pieces_ref,
    total_ref,
    grads_ref,
    pre_ref,
    act_ref,
    out_ref,
):
    slots = slots_ref.shape[0]
    ocean_blocks = goal_ref.shape[0]
    hidden, channels = w_in_t_ref.shape
    cells = slots_ref.shape[2]
    group = math.gcd(ocean_blocks, 4)
    chunk = math.gcd(hidden, 256)
    total_ref[...] = jnp.zeros_like(total_ref)
    grads_ref[...] = jnp.zeros_like(grads_ref)
    out_ref[...] = jnp.zeros_like(out_ref)

    batch = math.gcd(slots, 8)

    @pl.loop(0, slots // batch)
    def _(step):
        places = [step * batch + b for b in range(batch)]
        pieces = [
            jnp.dot(
                states_ref[state_at_ref[slot]], slots_ref[slot], preferred_element_type=jnp.float32
            ).astype(jnp.bfloat16)
            for slot in places
        ]
        for slot, piece in zip(places, pieces):
            total_ref[id_ref[slot]] += piece.astype(jnp.float32)

    @pl.loop(0, ocean_blocks // group)
    def _(step):
        first = step * group
        feat = jnp.concatenate(
            [total_ref[first + g].astype(jnp.bfloat16) for g in range(group)], axis=1
        )
        predicted = jnp.zeros((8, group * cells), jnp.float32)
        for h in range(0, hidden, chunk):
            rows = slice(h, h + chunk)
            pre = jnp.dot(w_in_t_ref[rows], feat, preferred_element_type=jnp.float32)
            pre_ref[rows] = pre
            act = (pre * jax.nn.sigmoid(pre)).astype(jnp.bfloat16)
            act_ref[rows] = act
            predicted += jnp.dot(w_out_t_ref[:, rows], act, preferred_element_type=jnp.float32)
        goal = jnp.concatenate([goal_ref[first + g] for g in range(group)], axis=1)
        mask = jnp.concatenate([mask_ref[first + g] for g in range(group)], axis=1)
        misfit = mask * (predicted - goal)
        high = misfit.astype(jnp.bfloat16).astype(jnp.float32)
        rest = misfit - high
        middle = rest.astype(jnp.bfloat16).astype(jnp.float32)
        low = rest - middle
        misfit_3 = jnp.concatenate([high, middle, low, jnp.zeros_like(low)], axis=0).astype(
            jnp.bfloat16
        )
        feat_grad = jnp.zeros((channels, group * cells), jnp.float32)
        for h in range(0, hidden, chunk):
            rows = slice(h, h + chunk)
            act_grad = jnp.dot(w_out_3_ref[rows], misfit_3, preferred_element_type=jnp.float32)
            pre = pre_ref[rows]
            gate = jax.nn.sigmoid(pre)
            pre_grad = (act_grad * gate * (1.0 + pre * (1.0 - gate))).astype(jnp.bfloat16)
            feat_grad += jnp.dot(w_in_ref[:, rows], pre_grad, preferred_element_type=jnp.float32)
            grads_ref[:, rows] += lax.dot_general(
                feat, pre_grad, (((1,), (1,)), ((), ())), preferred_element_type=jnp.float32
            )
            out_ref[:, rows] += lax.dot_general(
                misfit_3, act_ref[rows], (((1,), (1,)), ((), ())), preferred_element_type=jnp.float32
            )
        for g in range(group):
            grad_ref[first + g] = feat_grad[:, g * cells : (g + 1) * cells].astype(jnp.bfloat16)

    out = scale_out * (out_ref[0:8] + out_ref[8:16] + out_ref[16:24])
    for p in range(pieces_ref.shape[0]):
        pieces_ref[p, :, 0:hidden] = scale_in * grads_ref[8 * p : 8 * p + 8]
        if (p + 1) * 128 <= hidden:
            pieces_ref[p, :, hidden : hidden + 128] = out[:, p * 128 : (p + 1) * 128]
        else:
            pieces_ref[p, :, hidden : hidden + 128] = jnp.zeros((8, 128), jnp.float32)


def network(states, tiles, state_at, ids, wet_mask, target, w_in, w_out, scale_in, scale_out):
    _, channels, cells = states.shape
    ocean_blocks, outputs, _ = target.shape
    hidden = w_in.shape[1]
    group = math.gcd(ocean_blocks, 4)
    padded = jnp.pad(w_out, ((0, 0), (0, 8 - outputs)))
    whole = pl.BlockSpec(memory_space=pltpu.VMEM)
    return pl.pallas_call(
        lambda *refs: network_kernel(scale_in, scale_out, *refs),
        out_shape=(
            jax.ShapeDtypeStruct((ocean_blocks, channels, cells), jnp.bfloat16),
            jax.ShapeDtypeStruct((channels // 8, 8, hidden + 128), jnp.float32),
        ),
        in_specs=[pl.BlockSpec(memory_space=pltpu.SMEM)] * 2 + [whole] * 8,
        out_specs=(whole, whole),
        scratch_shapes=[
            pltpu.VMEM((ocean_blocks + 1, channels, cells), jnp.float32),
            pltpu.VMEM((channels, hidden), jnp.float32),
            pltpu.VMEM((hidden, group * cells), jnp.float32),
            pltpu.VMEM((hidden, group * cells), jnp.bfloat16),
            pltpu.VMEM((32, hidden), jnp.float32),
        ],
        compiler_params=pltpu.CompilerParams(vmem_limit_bytes=VMEM_BYTES),
    )(
        ids,
        state_at,
        states,
        tiles,
        wet_mask.astype(jnp.float32)[:, None, :],
        jnp.pad(target, ((0, 0), (0, 8 - outputs), (0, 0))),
        w_in,
        w_in.T,
        padded.T,
        jnp.concatenate([padded, padded, padded, jnp.zeros_like(padded)], axis=1),
    )


CHUNKS = 2
MESH = pl.DeviceIdType.MESH


def exchange_kernel(
    space_size,
    member_size,
    feat_ref,
    grads_ref,
    all_ref,
    sums_ref,
    inbox,
    total,
    term_send,
    term_recv,
    sum_send,
    sum_recv,
    line_send,
    line_recv,
    pair_send,
    pair_recv,
    own_sem,
):
    space, member = lax.axis_index("space"), lax.axis_index("member")
    ranks = space_size * member_size
    rank = member * space_size + space
    length = space_size // 2
    place, core = space // 2, space % 2
    size = feat_ref.shape[0] // CHUNKS

    def peer(i):
        other = lax.rem(rank + i, ranks)
        return other, {"space": other % space_size, "member": other // space_size}

    barrier = pltpu.get_barrier_semaphore()
    for i in range(1, ranks):
        pl.semaphore_signal(barrier, inc=1, device_id=peer(i)[1], device_id_type=MESH)
    pl.semaphore_wait(barrier, ranks - 1)

    def term(i):
        other, device = peer(i)
        return pltpu.make_async_remote_copy(
            src_ref=grads_ref.at[other],
            dst_ref=inbox.at[i - 1],
            send_sem=term_send.at[i - 1],
            recv_sem=term_recv.at[i - 1],
            device_id=device,
            device_id_type=MESH,
        )

    def piece(i, owner):
        return pltpu.make_async_remote_copy(
            src_ref=total,
            dst_ref=sums_ref.at[owner],
            send_sem=sum_send.at[i - 1],
            recv_sem=sum_recv.at[i - 1],
            device_id=peer(i)[1],
            device_id_type=MESH,
        )

    def source(origin, own, c):
        rows = pl.ds(c * size, size)
        return feat_ref.at[rows] if own else all_ref.at[origin, rows]

    def line(way, hop, c, origin, own):
        step = 1 if way == 0 else -1
        return pltpu.make_async_remote_copy(
            src_ref=source(origin, own, c),
            dst_ref=all_ref.at[origin, pl.ds(c * size, size)],
            send_sem=line_send.at[way, hop, c],
            recv_sem=line_recv.at[way, hop, c],
            device_id={"space": (place + step) * 2 + core},
            device_id_type=MESH,
        )

    def pair(index, c, origin, own):
        return pltpu.make_async_remote_copy(
            src_ref=source(origin, own, c),
            dst_ref=all_ref.at[origin, pl.ds(c * size, size)],
            send_sem=pair_send.at[index, c],
            recv_sem=pair_recv.at[index, c],
            device_id={"space": place * 2 + 1 - core},
            device_id_type=MESH,
        )

    def behind(way, hop):
        at = place - 1 - hop if way == 0 else place + 1 + hop
        return at, (at >= 0 if way == 0 else at < length)

    ahead = (place < length - 1, place > 0)
    own_copy = pltpu.make_async_copy(feat_ref, all_ref.at[space], own_sem.at[0])
    for c in range(CHUNKS):
        for way in range(2):

            @pl.when(ahead[way])
            def _():
                line(way, 0, c, space, True).start()

    for i in range(1, ranks):
        term(i).start()
    for c in range(CHUNKS):
        pair(0, c, space, True).start()
    own_copy.start()

    for hop in range(length - 1):
        for c in range(CHUNKS):
            for way in range(2):
                at, there = behind(way, hop)
                origin = at * 2 + core

                @pl.when(there)
                def _():
                    line(way, hop, c, origin, False).wait_recv()
                    if hop + 1 < length - 1:

                        @pl.when(ahead[way])
                        def _():
                            line(way, hop + 1, c, origin, False).start()

                    pair(1 + way * (length - 1) + hop, c, origin, False).start()

        if hop == 0:
            for i in range(1, ranks):
                term(i).wait_recv()
            value = grads_ref[rank]
            for i in range(1, ranks):
                value += inbox[i - 1]
            total[...] = value
            for i in range(1, ranks):
                piece(i, rank).start()
            own_sum = pltpu.make_async_copy(total, sums_ref.at[rank], own_sem.at[1])
            own_sum.start()

    own_copy.wait()
    own_sum.wait()
    for i in range(1, ranks):
        piece(i, lax.rem(rank + ranks - i, ranks)).wait_recv()
        piece(i, rank).wait_send()
        term(i).wait_send()
    for c in range(CHUNKS):
        pair(0, c, space, True).wait_send()
        pair(0, c, place * 2 + 1 - core, False).wait_recv()
        for way in range(2):

            @pl.when(ahead[way])
            def _():
                line(way, 0, c, space, True).wait_send()

            for hop in range(length - 1):
                at, there = behind(way, hop)
                origin = at * 2 + core
                index = 1 + way * (length - 1) + hop

                @pl.when(there)
                def _():
                    if hop + 1 < length - 1:

                        @pl.when(ahead[way])
                        def _():
                            line(way, hop + 1, c, origin, False).wait_send()

                    pair(index, c, origin, False).wait_send()
                    pair(index, c, at * 2 + 1 - core, False).wait_recv()


def exchange(feat_grad, grads, space_size, member_size):
    peers = space_size * member_size - 1
    hops = max(1, space_size // 2 - 1)
    dma = pltpu.SemaphoreType.DMA
    anywhere = pl.BlockSpec(memory_space=pl.ANY)
    return pl.pallas_call(
        lambda *refs: exchange_kernel(space_size, member_size, *refs),
        out_shape=(
            jax.ShapeDtypeStruct((space_size,) + feat_grad.shape, feat_grad.dtype),
            jax.ShapeDtypeStruct(grads.shape, grads.dtype),
        ),
        in_specs=[anywhere, pl.BlockSpec(memory_space=pltpu.VMEM)],
        out_specs=(anywhere, anywhere),
        scratch_shapes=[
            pltpu.VMEM((peers,) + grads.shape[1:], grads.dtype),
            pltpu.VMEM(grads.shape[1:], grads.dtype),
            dma((peers,)),
            dma((peers,)),
            dma((peers,)),
            dma((peers,)),
            dma((2, hops, CHUNKS)),
            dma((2, hops, CHUNKS)),
            dma((1 + 2 * hops, CHUNKS)),
            dma((1 + 2 * hops, CHUNKS)),
            dma((2,)),
        ],
        compiler_params=pltpu.CompilerParams(
            collective_id=0, has_side_effects=True, vmem_limit_bytes=VMEM_BYTES
        ),
    )(feat_grad, grads)


def spread_kernel(
    space_size,
    columns,
    member_size,
    state_ref,
    tiles_ref,
    states_ref,
    slots_ref,
    tile_send,
    tile_recv,
    share_send,
    share_recv,
    line_send,
    line_recv,
    pair_send,
    pair_recv,
    own_sem,
):
    group, space, member = (lax.axis_index(name) for name in ("group", "space", "member"))
    column = group * member_size + member
    length = space_size // 2
    place, core = space // 2, space % 2
    size = state_ref.shape[0] // CHUNKS
    share = tiles_ref.shape[1]

    def along(j):
        return lax.rem(space + j, space_size)

    def across(i):
        other = lax.rem(column + i, columns)
        return other, {"group": other // member_size, "member": other % member_size}

    barrier = pltpu.get_barrier_semaphore()
    for j in range(1, space_size):
        pl.semaphore_signal(barrier, inc=1, device_id={"space": along(j)}, device_id_type=MESH)
    for i in range(1, columns):
        pl.semaphore_signal(barrier, inc=1, device_id=across(i)[1], device_id_type=MESH)
    pl.semaphore_wait(barrier, space_size + columns - 2)

    def part(origin, owner):
        return slots_ref.at[origin, pl.ds(owner * share, share)]

    def tile(j, origin):
        return pltpu.make_async_remote_copy(
            src_ref=tiles_ref.at[along(j)],
            dst_ref=part(origin, column),
            send_sem=tile_send.at[j - 1],
            recv_sem=tile_recv.at[j - 1],
            device_id={"space": along(j)},
            device_id_type=MESH,
        )

    def shared(i, j, owner):
        origin = along(space_size - j)
        return pltpu.make_async_remote_copy(
            src_ref=tiles_ref.at[space] if j == 0 else part(origin, column),
            dst_ref=part(origin, owner),
            send_sem=share_send.at[i - 1, j],
            recv_sem=share_recv.at[i - 1, j],
            device_id=across(i)[1],
            device_id_type=MESH,
        )

    def source(origin, own, c):
        rows = pl.ds(c * size, size)
        return state_ref.at[rows] if own else states_ref.at[origin, rows]

    def line(way, hop, c, origin, own):
        step = 1 if way == 0 else -1
        return pltpu.make_async_remote_copy(
            src_ref=source(origin, own, c),
            dst_ref=states_ref.at[origin, pl.ds(c * size, size)],
            send_sem=line_send.at[way, hop, c],
            recv_sem=line_recv.at[way, hop, c],
            device_id={"space": (place + step) * 2 + core},
            device_id_type=MESH,
        )

    def pair(index, c, origin, own):
        return pltpu.make_async_remote_copy(
            src_ref=source(origin, own, c),
            dst_ref=states_ref.at[origin, pl.ds(c * size, size)],
            send_sem=pair_send.at[index, c],
            recv_sem=pair_recv.at[index, c],
            device_id={"space": place * 2 + 1 - core},
            device_id_type=MESH,
        )

    def behind(way, hop):
        at = place - 1 - hop if way == 0 else place + 1 + hop
        return at, (at >= 0 if way == 0 else at < length)

    ahead = (place < length - 1, place > 0)
    for j in range(1, space_size):
        tile(j, space).start()
    own_state = pltpu.make_async_copy(state_ref, states_ref.at[space], own_sem.at[0])
    own_tiles = pltpu.make_async_copy(tiles_ref.at[space], part(space, column), own_sem.at[1])
    for i in range(1, columns):
        shared(i, 0, column).start()
    for c in range(CHUNKS):
        for way in range(2):

            @pl.when(ahead[way])
            def _():
                line(way, 0, c, space, True).start()

        pair(0, c, space, True).start()
    own_state.start()
    own_tiles.start()

    order = list(range(1, space_size))
    hops = length - 1
    for hop in range(hops):
        for j in order[hop * len(order) // hops : (hop + 1) * len(order) // hops]:
            tile(j, along(space_size - j)).wait_recv()
            for i in range(1, columns):
                shared(i, j, column).start()
        for c in range(CHUNKS):
            for way in range(2):
                at, there = behind(way, hop)
                origin = at * 2 + core

                @pl.when(there)
                def _():
                    line(way, hop, c, origin, False).wait_recv()
                    if hop + 1 < hops:

                        @pl.when(ahead[way])
                        def _():
                            line(way, hop + 1, c, origin, False).start()

                    pair(1 + way * hops + hop, c, origin, False).start()

    own_state.wait()
    own_tiles.wait()
    for j in range(1, space_size):
        tile(j, space).wait_send()
    for i in range(1, columns):
        for j in range(space_size):
            shared(i, j, across(columns - i)[0]).wait_recv()
            shared(i, j, column).wait_send()
    for c in range(CHUNKS):
        pair(0, c, space, True).wait_send()
        pair(0, c, place * 2 + 1 - core, False).wait_recv()
        for way in range(2):

            @pl.when(ahead[way])
            def _():
                line(way, 0, c, space, True).wait_send()

            for hop in range(hops):
                at, there = behind(way, hop)
                origin = at * 2 + core
                index = 1 + way * hops + hop

                @pl.when(there)
                def _():
                    if hop + 1 < hops:

                        @pl.when(ahead[way])
                        def _():
                            line(way, hop + 1, c, origin, False).wait_send()

                    pair(index, c, origin, False).wait_send()
                    pair(index, c, at * 2 + 1 - core, False).wait_recv()


def spread(state, tile_slots, space_size, columns, member_size):
    hops = space_size // 2 - 1
    _, share, cells, _ = tile_slots.shape
    dma = pltpu.SemaphoreType.DMA
    anywhere = pl.BlockSpec(memory_space=pl.ANY)
    return pl.pallas_call(
        lambda *refs: spread_kernel(space_size, columns, member_size, *refs),
        out_shape=(
            jax.ShapeDtypeStruct((space_size,) + state.shape, state.dtype),
            jax.ShapeDtypeStruct((space_size, columns * share, cells, cells), tile_slots.dtype),
        ),
        in_specs=[anywhere, anywhere],
        out_specs=(anywhere, anywhere),
        scratch_shapes=[
            dma((space_size - 1,)),
            dma((space_size - 1,)),
            dma((columns - 1, space_size)),
            dma((columns - 1, space_size)),
            dma((2, hops, CHUNKS)),
            dma((2, hops, CHUNKS)),
            dma((1 + 2 * hops, CHUNKS)),
            dma((1 + 2 * hops, CHUNKS)),
            dma((2,)),
        ],
        compiler_params=pltpu.CompilerParams(
            collective_id=1, has_side_effects=True, vmem_limit_bytes=VMEM_BYTES
        ),
    )(state, tile_slots)


def fused_body(atm_state, remap_tiles, dest_device, dest_block, wet_mask, target, w_in, w_out):
    space_size = lax.axis_size("space")
    member_size = lax.axis_size("member")
    atm_blocks, top_count, cells, _ = remap_tiles.shape
    ocean_blocks = wet_mask.shape[0]
    channels = atm_state.shape[2]
    pieces_fit = channels == 8 * space_size * member_size and w_in.shape[1] <= 16 * channels
    columns = lax.axis_size("group") * member_size
    capacity = min(atm_blocks, max(2, 2 * atm_blocks * top_count // space_size))
    if not pieces_fit or ocean_blocks % CHUNKS or atm_blocks % CHUNKS or capacity % columns:
        return general_body(
            atm_state, remap_tiles, dest_device, dest_block, wet_mask, target, w_in, w_out
        )
    pair_count = atm_blocks * top_count
    slot_total = space_size * capacity
    dest_flat = dest_device.reshape(pair_count)
    onehot = (dest_flat[:, None] == jnp.arange(space_size, dtype=jnp.int32)[None, :]).astype(
        jnp.int32
    )
    slot_rank = jnp.sum((jnp.cumsum(onehot, axis=0) - onehot) * onehot, axis=1)
    slot_index = dest_flat * capacity + slot_rank
    codes = (
        jnp.full((slot_total,), ocean_blocks * pair_count, jnp.int32)
        .at[slot_index]
        .set(dest_block.reshape(pair_count) * pair_count + jnp.arange(pair_count, dtype=jnp.int32))
    ).reshape(space_size, capacity)
    share = capacity // columns
    column = lax.axis_index("group") * member_size + lax.axis_index("member")
    mine = lax.dynamic_slice_in_dim(codes, column * share, share, axis=1)
    tile_slots = slotted_tiles(
        (mine % pair_count).reshape(-1), remap_tiles.reshape(pair_count, cells, cells)
    ).reshape(space_size, share, cells, cells)
    received_codes = lax.all_to_all(codes, "space", split_axis=0, concat_axis=0, tiled=True)
    states, tiles = spread(atm_state[0], tile_slots, space_size, columns, member_size)
    received_ids = (received_codes // pair_count).reshape(slot_total)
    state_at = (
        jnp.arange(space_size, dtype=jnp.int32)[:, None] * atm_blocks
        + received_codes % pair_count // top_count
    ).reshape(slot_total)
    cell_total = member_size * space_size * ocean_blocks * cells
    scale_in = math.sqrt(w_in.shape[1] / cell_total)
    scale_out = 1.0 / math.sqrt(cell_total)
    feat_grad, grads = network(
        states.reshape(space_size * atm_blocks, channels, cells),
        tiles.reshape(slot_total, cells, cells),
        state_at,
        received_ids,
        wet_mask,
        target[0],
        w_in,
        w_out,
        scale_in,
        scale_out,
    )
    gathered, summed = exchange(feat_grad, grads, space_size, member_size)
    owner = dest_flat * ocean_blocks + dest_block.reshape(pair_count)
    adjoint = adjoint_of(
        owner, gathered.reshape(space_size * ocean_blocks, channels, cells), remap_tiles
    )
    hidden, outputs = w_out.shape
    grad_in = summed[:, :, :hidden].reshape(channels, hidden)
    grad_out = summed[: hidden // 128, :outputs, hidden:]
    return (adjoint[None], grad_in, grad_out.transpose(0, 2, 1).reshape(hidden, outputs))


def solution(mesh):
    body = fused_body if mesh.shape["level"] == 1 and mesh.shape["space"] in (4, 6, 8) else general_body
    return jax.shard_map(
        body,
        mesh=mesh,
        in_specs=(
            P("member", ("group", "space"), None, None),
            P("space", None, None, None),
            P("space", None),
            P("space", None),
            P("space", None),
            P("member", ("group", "space"), None, None),
            P(None, "level"),
            P("level", None),
        ),
        out_specs=(
            P("member", ("group", "space"), "level", None),
            P("group", "level"),
            P("level", "group"),
        ),
        check_vma=False,
    )
```

```python
import math

import jax
import jax.numpy as jnp
from jax import lax
from jax.experimental import pallas as pl
from jax.experimental.pallas import tpu as pltpu
from jax.sharding import PartitionSpec as P


def remap_pieces(source, remap_tiles, slot_index, slot_total):
    pieces = jnp.einsum(
        "aci,akij->akcj", source, remap_tiles, preferred_element_type=jnp.float32
    ).astype(jnp.bfloat16)
    pair_count = pieces.shape[0] * pieces.shape[1]
    pieces = pieces.reshape(pair_count, source.shape[1], source.shape[2])
    return (
        jnp.zeros((slot_total, source.shape[1], source.shape[2]), jnp.bfloat16)
        .at[slot_index]
        .set(pieces)
    )


def add_pieces(received, received_ids, ocean_blocks):
    flat_data = received.reshape(-1, received.shape[2], received.shape[3]).astype(jnp.float32)
    summed = jnp.zeros((ocean_blocks + 1, received.shape[2], received.shape[3]), jnp.float32)
    summed = summed.at[received_ids.reshape(-1)].add(flat_data)
    return summed[:ocean_blocks].astype(jnp.bfloat16)


def general_body(atm_state, remap_tiles, dest_device, dest_block, wet_mask, target, w_in, w_out):
    space_size = lax.axis_size("space")
    member_size = lax.axis_size("member")
    level_size = lax.axis_size("level")
    atm_blocks, top_count, cells, _ = remap_tiles.shape
    ocean_blocks = wet_mask.shape[0]
    channels = atm_state.shape[2]
    half_chan = channels // level_size
    capacity = min(atm_blocks, max(2, 2 * atm_blocks * top_count // space_size))
    pair_count = atm_blocks * top_count
    slot_total = space_size * capacity
    dest_flat = dest_device.reshape(pair_count)
    onehot = (dest_flat[:, None] == jnp.arange(space_size, dtype=jnp.int32)[None, :]).astype(
        jnp.int32
    )
    slot_rank = jnp.sum((jnp.cumsum(onehot, axis=0) - onehot) * onehot, axis=1)
    slot_index = dest_flat * capacity + slot_rank
    send_ids = (
        jnp.full((slot_total,), ocean_blocks, jnp.int32)
        .at[slot_index]
        .set(dest_block.reshape(pair_count))
    )
    send_ids = send_ids.reshape(space_size, capacity)
    local_state = atm_state[0]
    outgoing = remap_pieces(local_state, remap_tiles, slot_index, slot_total).reshape(
        space_size, capacity, channels, cells
    )
    received, received_ids = (
        lax.all_to_all(outgoing, "space", split_axis=0, concat_axis=0, tiled=True),
        lax.all_to_all(send_ids, "space", split_axis=0, concat_axis=0, tiled=True),
    )
    features = add_pieces(received, received_ids, ocean_blocks)
    pre_act = jnp.einsum("ch,ocj->ohj", w_in, features, preferred_element_type=jnp.float32)
    activated = jax.nn.silu(pre_act).astype(jnp.bfloat16)
    partial_flux = jnp.einsum("hq,ohj->oqj", w_out, activated, preferred_element_type=jnp.float32)
    predicted = lax.psum(partial_flux, "level")
    misfit = wet_mask.astype(jnp.float32)[:, None, :] * (predicted - target[0])
    act_grad = jnp.einsum(
        "hq,oqj->ohj", w_out.astype(jnp.float32), misfit, precision=lax.Precision.HIGHEST
    )
    gate_value = jax.nn.sigmoid(pre_act)
    pre_grad = (act_grad * gate_value * (1.0 + pre_act * (1.0 - gate_value))).astype(jnp.bfloat16)
    feat_grad = lax.psum_scatter(
        jnp.einsum("ch,ohj->coj", w_in, pre_grad, preferred_element_type=jnp.float32),
        "level",
        scatter_dimension=0,
        tiled=True,
    ).astype(jnp.bfloat16)
    reply = jnp.take(feat_grad, received_ids.reshape(-1), axis=1, mode="clip")
    reply = reply.reshape(half_chan, space_size, capacity, cells)
    returned = lax.all_to_all(reply, "space", split_axis=1, concat_axis=1, tiled=True)
    pair_grad = jnp.take(returned.reshape(half_chan, slot_total, cells), slot_index, axis=1)
    pair_grad = pair_grad.reshape(half_chan, atm_blocks, top_count, cells)
    adjoint = jnp.einsum(
        "cakj,akij->aci", pair_grad, remap_tiles, preferred_element_type=jnp.float32
    )
    cell_total = member_size * space_size * ocean_blocks * cells
    scale_in = math.sqrt(w_in.shape[1] * level_size / cell_total)
    scale_out = 1.0 / math.sqrt(cell_total)
    grad_in = scale_in * jnp.einsum(
        "ocj,ohj->ch", features, pre_grad, preferred_element_type=jnp.float32
    )
    grad_out = scale_out * jnp.einsum(
        "ohj,oqj->hq",
        activated,
        misfit,
        preferred_element_type=jnp.float32,
        precision=lax.Precision.HIGHEST,
    )
    grad_in, grad_out = lax.psum((grad_in, grad_out), ("space", "member"))
    return (adjoint[None], grad_in, grad_out)


VMEM_BYTES = 48 * 1024 * 1024


def slots_kernel(pair_ref, tiles_ref, out_ref):
    @pl.loop(0, out_ref.shape[0], unroll=4)
    def _(slot):
        out_ref[slot] = tiles_ref[pair_ref[slot]]


def slotted_tiles(pairs, tiles):
    whole = pl.BlockSpec(memory_space=pltpu.VMEM)
    return pl.pallas_call(
        slots_kernel,
        out_shape=jax.ShapeDtypeStruct(pairs.shape + tiles.shape[1:], tiles.dtype),
        in_specs=[pl.BlockSpec(memory_space=pltpu.SMEM), whole],
        out_specs=whole,
        compiler_params=pltpu.CompilerParams(vmem_limit_bytes=VMEM_BYTES),
    )(pairs, tiles)


def adjoint_kernel(slot_ref, back_ref, tiles_ref, out_ref):
    step = pl.program_id(0)
    blocks, top_count = tiles_ref.shape[:2]
    for a in range(blocks):
        first = (step * blocks + a) * top_count
        grads = jnp.concatenate([back_ref[slot_ref[first + k]] for k in range(top_count)], axis=1)
        wide = jnp.concatenate([tiles_ref[a, k] for k in range(top_count)], axis=1)
        out_ref[a] = lax.dot_general(
            grads, wide, (((1,), (1,)), ((), ())), preferred_element_type=jnp.float32
        )


def adjoint_of(slot_index, returned, tiles):
    atm_blocks, top_count, cells, _ = tiles.shape
    slots, channels, _ = returned.shape
    per_step = math.gcd(atm_blocks, 4)
    return pl.pallas_call(
        adjoint_kernel,
        out_shape=jax.ShapeDtypeStruct((atm_blocks, channels, cells), jnp.float32),
        grid_spec=pltpu.PrefetchScalarGridSpec(
            num_scalar_prefetch=1,
            grid=(atm_blocks // per_step,),
            in_specs=[
                pl.BlockSpec((slots, channels, cells), lambda s, _: (0, 0, 0)),
                pl.BlockSpec((per_step, top_count, cells, cells), lambda s, _: (s, 0, 0, 0)),
            ],
            out_specs=pl.BlockSpec((per_step, channels, cells), lambda s, _: (s, 0, 0)),
        ),
        compiler_params=pltpu.CompilerParams(vmem_limit_bytes=VMEM_BYTES),
    )(slot_index, returned, tiles)


def network_kernel(
    scale_in,
    scale_out,
    id_ref,
    state_at_ref,
    states_ref,
    slots_ref,
    mask_ref,
    goal_ref,
    w_in_ref,
    w_in_t_ref,
    w_out_t_ref,
    w_out_3_ref,
    grad_ref,
    pieces_ref,
    total_ref,
    grads_ref,
    pre_ref,
    act_ref,
    out_ref,
):
    slots = slots_ref.shape[0]
    ocean_blocks = goal_ref.shape[0]
    hidden, channels = w_in_t_ref.shape
    cells = slots_ref.shape[2]
    group = math.gcd(ocean_blocks, 4)
    chunk = math.gcd(hidden, 256)
    total_ref[...] = jnp.zeros_like(total_ref)
    grads_ref[...] = jnp.zeros_like(grads_ref)
    out_ref[...] = jnp.zeros_like(out_ref)

    batch = math.gcd(slots, 8)

    @pl.loop(0, slots // batch)
    def _(step):
        places = [step * batch + b for b in range(batch)]
        pieces = [
            jnp.dot(
                states_ref[state_at_ref[slot]], slots_ref[slot], preferred_element_type=jnp.float32
            ).astype(jnp.bfloat16)
            for slot in places
        ]
        for slot, piece in zip(places, pieces):
            total_ref[id_ref[slot]] += piece.astype(jnp.float32)

    @pl.loop(0, ocean_blocks // group)
    def _(step):
        first = step * group
        feat = jnp.concatenate(
            [total_ref[first + g].astype(jnp.bfloat16) for g in range(group)], axis=1
        )
        predicted = jnp.zeros((8, group * cells), jnp.float32)
        for h in range(0, hidden, chunk):
            rows = slice(h, h + chunk)
            pre = jnp.dot(w_in_t_ref[rows], feat, preferred_element_type=jnp.float32)
            pre_ref[rows] = pre
            act = (pre * jax.nn.sigmoid(pre)).astype(jnp.bfloat16)
            act_ref[rows] = act
            predicted += jnp.dot(w_out_t_ref[:, rows], act, preferred_element_type=jnp.float32)
        goal = jnp.concatenate([goal_ref[first + g] for g in range(group)], axis=1)
        mask = jnp.concatenate([mask_ref[first + g] for g in range(group)], axis=1)
        misfit = mask * (predicted - goal)
        high = misfit.astype(jnp.bfloat16).astype(jnp.float32)
        rest = misfit - high
        middle = rest.astype(jnp.bfloat16).astype(jnp.float32)
        low = rest - middle
        misfit_3 = jnp.concatenate([high, middle, low, jnp.zeros_like(low)], axis=0).astype(
            jnp.bfloat16
        )
        feat_grad = jnp.zeros((channels, group * cells), jnp.float32)
        for h in range(0, hidden, chunk):
            rows = slice(h, h + chunk)
            act_grad = jnp.dot(w_out_3_ref[rows], misfit_3, preferred_element_type=jnp.float32)
            pre = pre_ref[rows]
            gate = jax.nn.sigmoid(pre)
            pre_grad = (act_grad * gate * (1.0 + pre * (1.0 - gate))).astype(jnp.bfloat16)
            feat_grad += jnp.dot(w_in_ref[:, rows], pre_grad, preferred_element_type=jnp.float32)
            grads_ref[:, rows] += lax.dot_general(
                feat, pre_grad, (((1,), (1,)), ((), ())), preferred_element_type=jnp.float32
            )
            out_ref[:, rows] += lax.dot_general(
                misfit_3, act_ref[rows], (((1,), (1,)), ((), ())), preferred_element_type=jnp.float32
            )
        for g in range(group):
            grad_ref[first + g] = feat_grad[:, g * cells : (g + 1) * cells].astype(jnp.bfloat16)

    out = scale_out * (out_ref[0:8] + out_ref[8:16] + out_ref[16:24])
    for p in range(pieces_ref.shape[0]):
        pieces_ref[p, :, 0:hidden] = scale_in * grads_ref[8 * p : 8 * p + 8]
        if (p + 1) * 128 <= hidden:
            pieces_ref[p, :, hidden : hidden + 128] = out[:, p * 128 : (p + 1) * 128]
        else:
            pieces_ref[p, :, hidden : hidden + 128] = jnp.zeros((8, 128), jnp.float32)


def network(states, tiles, state_at, ids, wet_mask, target, w_in, w_out, scale_in, scale_out):
    _, channels, cells = states.shape
    ocean_blocks, outputs, _ = target.shape
    hidden = w_in.shape[1]
    group = math.gcd(ocean_blocks, 4)
    padded = jnp.pad(w_out, ((0, 0), (0, 8 - outputs)))
    whole = pl.BlockSpec(memory_space=pltpu.VMEM)
    return pl.pallas_call(
        lambda *refs: network_kernel(scale_in, scale_out, *refs),
        out_shape=(
            jax.ShapeDtypeStruct((ocean_blocks, channels, cells), jnp.bfloat16),
            jax.ShapeDtypeStruct((channels // 8, 8, hidden + 128), jnp.float32),
        ),
        in_specs=[pl.BlockSpec(memory_space=pltpu.SMEM)] * 2 + [whole] * 8,
        out_specs=(whole, whole),
        scratch_shapes=[
            pltpu.VMEM((ocean_blocks + 1, channels, cells), jnp.float32),
            pltpu.VMEM((channels, hidden), jnp.float32),
            pltpu.VMEM((hidden, group * cells), jnp.float32),
            pltpu.VMEM((hidden, group * cells), jnp.bfloat16),
            pltpu.VMEM((32, hidden), jnp.float32),
        ],
        compiler_params=pltpu.CompilerParams(vmem_limit_bytes=VMEM_BYTES),
    )(
        ids,
        state_at,
        states,
        tiles,
        wet_mask.astype(jnp.float32)[:, None, :],
        jnp.pad(target, ((0, 0), (0, 8 - outputs), (0, 0))),
        w_in,
        w_in.T,
        padded.T,
        jnp.concatenate([padded, padded, padded, jnp.zeros_like(padded)], axis=1),
    )


CHUNKS = 2
MESH = pl.DeviceIdType.MESH


def exchange_kernel(
    space_size,
    member_size,
    feat_ref,
    grads_ref,
    all_ref,
    sums_ref,
    team_box,
    partial,
    place_box,
    total,
    team_send,
    team_recv,
    place_send,
    place_recv,
    line_send,
    line_recv,
    pair_send,
    pair_recv,
    own_sem,
):
    space, member = lax.axis_index("space"), lax.axis_index("member")
    length = space_size // 2
    place, core = space // 2, space % 2
    size = feat_ref.shape[0] // CHUNKS

    teams = 2 * member_size
    team = member * 2 + core

    def mate(i):
        other = lax.rem(team + i, teams)
        return other, {"space": place * 2 + other % 2, "member": other // 2}

    def far(i):
        other = lax.rem(place + i, length)
        return other, {"space": other * 2 + core}

    barrier = pltpu.get_barrier_semaphore()
    for i in range(1, teams):
        pl.semaphore_signal(barrier, inc=1, device_id=mate(i)[1], device_id_type=MESH)
    for i in range(1, length):
        pl.semaphore_signal(barrier, inc=1, device_id=far(i)[1], device_id_type=MESH)
    pl.semaphore_wait(barrier, teams + length - 2)

    def team_copy(back, i, owner):
        other, device = mate(i)
        rows = pl.ds((owner if back else other) * length, length)
        return pltpu.make_async_remote_copy(
            src_ref=sums_ref.at[rows] if back else grads_ref.at[rows],
            dst_ref=sums_ref.at[rows] if back else team_box.at[i - 1],
            send_sem=team_send.at[back, i - 1],
            recv_sem=team_recv.at[back, i - 1],
            device_id=device,
            device_id_type=MESH,
        )

    def place_copy(back, i, owner):
        other, device = far(i)
        return pltpu.make_async_remote_copy(
            src_ref=total if back else partial.at[other],
            dst_ref=sums_ref.at[team * length + owner] if back else place_box.at[i - 1],
            send_sem=place_send.at[back, i - 1],
            recv_sem=place_recv.at[back, i - 1],
            device_id=device,
            device_id_type=MESH,
        )

    own_sum = pltpu.make_async_copy(total, sums_ref.at[team * length + place], own_sem.at[1])

    def sum_team():
        for i in range(1, teams):
            team_copy(0, i, team).wait_recv()
        value = grads_ref[pl.ds(team * length, length)]
        for i in range(1, teams):
            value += team_box[i - 1]
        partial[...] = value
        for i in range(1, length):
            place_copy(0, i, place).start()

    def sum_places():
        for i in range(1, length):
            place_copy(0, i, place).wait_recv()
        value = partial[place]
        for i in range(1, length):
            value += place_box[i - 1]
        total[...] = value
        for i in range(1, length):
            place_copy(1, i, place).start()
        own_sum.start()

    def share_sums():
        for i in range(1, length):
            place_copy(1, i, far(length - i)[0]).wait_recv()
        own_sum.wait()
        for i in range(1, teams):
            team_copy(1, i, team).start()

    phases = [sum_team, sum_places, share_sums]

    def source(origin, own, c):
        rows = pl.ds(c * size, size)
        return feat_ref.at[rows] if own else all_ref.at[origin, rows]

    def line(way, hop, c, origin, own):
        step = 1 if way == 0 else -1
        return pltpu.make_async_remote_copy(
            src_ref=source(origin, own, c),
            dst_ref=all_ref.at[origin, pl.ds(c * size, size)],
            send_sem=line_send.at[way, hop, c],
            recv_sem=line_recv.at[way, hop, c],
            device_id={"space": (place + step) * 2 + core},
            device_id_type=MESH,
        )

    def pair(index, c, origin, own):
        return pltpu.make_async_remote_copy(
            src_ref=source(origin, own, c),
            dst_ref=all_ref.at[origin, pl.ds(c * size, size)],
            send_sem=pair_send.at[index, c],
            recv_sem=pair_recv.at[index, c],
            device_id={"space": place * 2 + 1 - core},
            device_id_type=MESH,
        )

    def behind(way, hop):
        at = place - 1 - hop if way == 0 else place + 1 + hop
        return at, (at >= 0 if way == 0 else at < length)

    ahead = (place < length - 1, place > 0)
    own_copy = pltpu.make_async_copy(feat_ref, all_ref.at[space], own_sem.at[0])
    for i in range(1, teams):
        team_copy(0, i, team).start()
    for c in range(CHUNKS):
        for way in range(2):

            @pl.when(ahead[way])
            def _():
                line(way, 0, c, space, True).start()

    for c in range(CHUNKS):
        pair(0, c, space, True).start()
    own_copy.start()

    for hop in range(length - 1):
        for c in range(CHUNKS):
            for way in range(2):
                at, there = behind(way, hop)
                origin = at * 2 + core

                @pl.when(there)
                def _():
                    line(way, hop, c, origin, False).wait_recv()
                    if hop + 1 < length - 1:

                        @pl.when(ahead[way])
                        def _():
                            line(way, hop + 1, c, origin, False).start()

                    pair(1 + way * (length - 1) + hop, c, origin, False).start()

            if phases:
                phases.pop(0)()

    own_copy.wait()
    for back in range(2):
        for i in range(1, teams):
            team_copy(back, i, team).wait_send()
        for i in range(1, length):
            place_copy(back, i, place).wait_send()
    for i in range(1, teams):
        team_copy(1, i, mate(teams - i)[0]).wait_recv()
    for c in range(CHUNKS):
        pair(0, c, space, True).wait_send()
        pair(0, c, place * 2 + 1 - core, False).wait_recv()
        for way in range(2):

            @pl.when(ahead[way])
            def _():
                line(way, 0, c, space, True).wait_send()

            for hop in range(length - 1):
                at, there = behind(way, hop)
                origin = at * 2 + core
                index = 1 + way * (length - 1) + hop

                @pl.when(there)
                def _():
                    if hop + 1 < length - 1:

                        @pl.when(ahead[way])
                        def _():
                            line(way, hop + 1, c, origin, False).wait_send()

                    pair(index, c, origin, False).wait_send()
                    pair(index, c, at * 2 + 1 - core, False).wait_recv()


def exchange(feat_grad, grads, space_size, member_size):
    teams, length = 2 * member_size, space_size // 2
    hops = length - 1
    piece = grads.shape[1:]
    dma = pltpu.SemaphoreType.DMA
    anywhere = pl.BlockSpec(memory_space=pl.ANY)
    return pl.pallas_call(
        lambda *refs: exchange_kernel(space_size, member_size, *refs),
        out_shape=(
            jax.ShapeDtypeStruct((space_size,) + feat_grad.shape, feat_grad.dtype),
            jax.ShapeDtypeStruct(grads.shape, grads.dtype),
        ),
        in_specs=[anywhere, pl.BlockSpec(memory_space=pltpu.VMEM)],
        out_specs=(anywhere, anywhere),
        scratch_shapes=[
            pltpu.VMEM((teams - 1, length) + piece, grads.dtype),
            pltpu.VMEM((length,) + piece, grads.dtype),
            pltpu.VMEM((length - 1,) + piece, grads.dtype),
            pltpu.VMEM(piece, grads.dtype),
            dma((2, teams - 1)),
            dma((2, teams - 1)),
            dma((2, length - 1)),
            dma((2, length - 1)),
            dma((2, hops, CHUNKS)),
            dma((2, hops, CHUNKS)),
            dma((1 + 2 * hops, CHUNKS)),
            dma((1 + 2 * hops, CHUNKS)),
            dma((2,)),
        ],
        compiler_params=pltpu.CompilerParams(
            collective_id=0, has_side_effects=True, vmem_limit_bytes=VMEM_BYTES
        ),
    )(feat_grad, grads)


def spread_kernel(
    space_size,
    columns,
    member_size,
    state_ref,
    tiles_ref,
    codes_ref,
    states_ref,
    slots_ref,
    all_codes_ref,
    code_send,
    code_recv,
    tile_send,
    tile_recv,
    share_send,
    share_recv,
    line_send,
    line_recv,
    pair_send,
    pair_recv,
    own_sem,
):
    group, space, member = (lax.axis_index(name) for name in ("group", "space", "member"))
    column = group * member_size + member
    length = space_size // 2
    place, core = space // 2, space % 2
    size = state_ref.shape[0] // CHUNKS
    share = tiles_ref.shape[1]

    def along(j):
        return lax.rem(space + j, space_size)

    def across(i):
        other = lax.rem(column + i, columns)
        return other, {"group": other // member_size, "member": other % member_size}

    barrier = pltpu.get_barrier_semaphore()
    for j in range(1, space_size):
        pl.semaphore_signal(barrier, inc=1, device_id={"space": along(j)}, device_id_type=MESH)
    for i in range(1, columns):
        pl.semaphore_signal(barrier, inc=1, device_id=across(i)[1], device_id_type=MESH)
    pl.semaphore_wait(barrier, space_size + columns - 2)

    def part(origin, owner):
        return slots_ref.at[origin, pl.ds(owner * share, share)]

    def tile(j, origin):
        return pltpu.make_async_remote_copy(
            src_ref=tiles_ref.at[along(j)],
            dst_ref=part(origin, column),
            send_sem=tile_send.at[j - 1],
            recv_sem=tile_recv.at[j - 1],
            device_id={"space": along(j)},
            device_id_type=MESH,
        )

    def code(j, origin):
        return pltpu.make_async_remote_copy(
            src_ref=codes_ref.at[along(j)],
            dst_ref=all_codes_ref.at[origin],
            send_sem=code_send.at[j - 1],
            recv_sem=code_recv.at[j - 1],
            device_id={"space": along(j)},
            device_id_type=MESH,
        )

    def shared(i, j, owner):
        origin = along(space_size - j)
        return pltpu.make_async_remote_copy(
            src_ref=tiles_ref.at[space] if j == 0 else part(origin, column),
            dst_ref=part(origin, owner),
            send_sem=share_send.at[i - 1, j],
            recv_sem=share_recv.at[i - 1, j],
            device_id=across(i)[1],
            device_id_type=MESH,
        )

    def source(origin, own, c):
        rows = pl.ds(c * size, size)
        return state_ref.at[rows] if own else states_ref.at[origin, rows]

    def line(way, hop, c, origin, own):
        step = 1 if way == 0 else -1
        return pltpu.make_async_remote_copy(
            src_ref=source(origin, own, c),
            dst_ref=states_ref.at[origin, pl.ds(c * size, size)],
            send_sem=line_send.at[way, hop, c],
            recv_sem=line_recv.at[way, hop, c],
            device_id={"space": (place + step) * 2 + core},
            device_id_type=MESH,
        )

    def pair(index, c, origin, own):
        return pltpu.make_async_remote_copy(
            src_ref=source(origin, own, c),
            dst_ref=states_ref.at[origin, pl.ds(c * size, size)],
            send_sem=pair_send.at[index, c],
            recv_sem=pair_recv.at[index, c],
            device_id={"space": place * 2 + 1 - core},
            device_id_type=MESH,
        )

    def behind(way, hop):
        at = place - 1 - hop if way == 0 else place + 1 + hop
        return at, (at >= 0 if way == 0 else at < length)

    ahead = (place < length - 1, place > 0)
    for j in range(1, space_size):
        code(j, space).start()
        tile(j, space).start()
    own_codes = pltpu.make_async_copy(codes_ref.at[space], all_codes_ref.at[space], own_sem.at[2])
    own_codes.start()
    own_state = pltpu.make_async_copy(state_ref, states_ref.at[space], own_sem.at[0])
    own_tiles = pltpu.make_async_copy(tiles_ref.at[space], part(space, column), own_sem.at[1])
    for i in range(1, columns):
        shared(i, 0, column).start()
    for c in range(CHUNKS):
        for way in range(2):

            @pl.when(ahead[way])
            def _():
                line(way, 0, c, space, True).start()

        pair(0, c, space, True).start()
    own_state.start()
    own_tiles.start()

    order = list(range(1, space_size))
    hops = length - 1
    for hop in range(hops):
        for j in order[hop * len(order) // hops : (hop + 1) * len(order) // hops]:
            tile(j, along(space_size - j)).wait_recv()
            for i in range(1, columns):
                shared(i, j, column).start()
        for c in range(CHUNKS):
            for way in range(2):
                at, there = behind(way, hop)
                origin = at * 2 + core

                @pl.when(there)
                def _():
                    line(way, hop, c, origin, False).wait_recv()
                    if hop + 1 < hops:

                        @pl.when(ahead[way])
                        def _():
                            line(way, hop + 1, c, origin, False).start()

                    pair(1 + way * hops + hop, c, origin, False).start()

    own_state.wait()
    own_tiles.wait()
    own_codes.wait()
    for j in range(1, space_size):
        code(j, along(space_size - j)).wait_recv()
        code(j, space).wait_send()
        tile(j, space).wait_send()
    for i in range(1, columns):
        for j in range(space_size):
            shared(i, j, across(columns - i)[0]).wait_recv()
            shared(i, j, column).wait_send()
    for c in range(CHUNKS):
        pair(0, c, space, True).wait_send()
        pair(0, c, place * 2 + 1 - core, False).wait_recv()
        for way in range(2):

            @pl.when(ahead[way])
            def _():
                line(way, 0, c, space, True).wait_send()

            for hop in range(hops):
                at, there = behind(way, hop)
                origin = at * 2 + core
                index = 1 + way * hops + hop

                @pl.when(there)
                def _():
                    if hop + 1 < hops:

                        @pl.when(ahead[way])
                        def _():
                            line(way, hop + 1, c, origin, False).wait_send()

                    pair(index, c, origin, False).wait_send()
                    pair(index, c, at * 2 + 1 - core, False).wait_recv()


def spread(state, tile_slots, codes, space_size, columns, member_size):
    hops = space_size // 2 - 1
    _, share, cells, _ = tile_slots.shape
    dma = pltpu.SemaphoreType.DMA
    anywhere = pl.BlockSpec(memory_space=pl.ANY)
    return pl.pallas_call(
        lambda *refs: spread_kernel(space_size, columns, member_size, *refs),
        out_shape=(
            jax.ShapeDtypeStruct((space_size,) + state.shape, state.dtype),
            jax.ShapeDtypeStruct((space_size, columns * share, cells, cells), tile_slots.dtype),
            jax.ShapeDtypeStruct(codes.shape, codes.dtype),
        ),
        in_specs=[anywhere] * 3,
        out_specs=(anywhere,) * 3,
        scratch_shapes=[
            dma((space_size - 1,)),
            dma((space_size - 1,)),
            dma((space_size - 1,)),
            dma((space_size - 1,)),
            dma((columns - 1, space_size)),
            dma((columns - 1, space_size)),
            dma((2, hops, CHUNKS)),
            dma((2, hops, CHUNKS)),
            dma((1 + 2 * hops, CHUNKS)),
            dma((1 + 2 * hops, CHUNKS)),
            dma((3,)),
        ],
        compiler_params=pltpu.CompilerParams(
            collective_id=1, has_side_effects=True, vmem_limit_bytes=VMEM_BYTES
        ),
    )(state, tile_slots, codes)


def fused_body(atm_state, remap_tiles, dest_device, dest_block, wet_mask, target, w_in, w_out):
    space_size = lax.axis_size("space")
    member_size = lax.axis_size("member")
    atm_blocks, top_count, cells, _ = remap_tiles.shape
    ocean_blocks = wet_mask.shape[0]
    channels = atm_state.shape[2]
    pieces_fit = channels == 8 * space_size * member_size and w_in.shape[1] <= 16 * channels
    columns = lax.axis_size("group") * member_size
    capacity = min(atm_blocks, max(2, 2 * atm_blocks * top_count // space_size))
    if not pieces_fit or ocean_blocks % CHUNKS or atm_blocks % CHUNKS or capacity % columns:
        return general_body(
            atm_state, remap_tiles, dest_device, dest_block, wet_mask, target, w_in, w_out
        )
    pair_count = atm_blocks * top_count
    slot_total = space_size * capacity
    dest_flat = dest_device.reshape(pair_count)
    onehot = (dest_flat[:, None] == jnp.arange(space_size, dtype=jnp.int32)[None, :]).astype(
        jnp.int32
    )
    slot_rank = jnp.sum((jnp.cumsum(onehot, axis=0) - onehot) * onehot, axis=1)
    slot_index = dest_flat * capacity + slot_rank
    codes = (
        jnp.full((slot_total,), ocean_blocks * pair_count, jnp.int32)
        .at[slot_index]
        .set(dest_block.reshape(pair_count) * pair_count + jnp.arange(pair_count, dtype=jnp.int32))
    ).reshape(space_size, capacity)
    share = capacity // columns
    column = lax.axis_index("group") * member_size + lax.axis_index("member")
    mine = lax.dynamic_slice_in_dim(codes, column * share, share, axis=1)
    tile_slots = slotted_tiles(
        (mine % pair_count).reshape(-1), remap_tiles.reshape(pair_count, cells, cells)
    ).reshape(space_size, share, cells, cells)
    wide_codes = jnp.broadcast_to(
        jnp.pad(codes, ((0, 0), (0, -capacity % 128)))[:, None, :], (space_size, 8, -(-capacity // 128) * 128)
    )
    states, tiles, received_codes = spread(
        atm_state[0], tile_slots, wide_codes, space_size, columns, member_size
    )
    received_codes = received_codes[:, 0, :capacity]
    received_ids = (received_codes // pair_count).reshape(slot_total)
    state_at = (
        jnp.arange(space_size, dtype=jnp.int32)[:, None] * atm_blocks
        + received_codes % pair_count // top_count
    ).reshape(slot_total)
    cell_total = member_size * space_size * ocean_blocks * cells
    scale_in = math.sqrt(w_in.shape[1] / cell_total)
    scale_out = 1.0 / math.sqrt(cell_total)
    feat_grad, grads = network(
        states.reshape(space_size * atm_blocks, channels, cells),
        tiles.reshape(slot_total, cells, cells),
        state_at,
        received_ids,
        wet_mask,
        target[0],
        w_in,
        w_out,
        scale_in,
        scale_out,
    )
    gathered, summed = exchange(feat_grad, grads, space_size, member_size)
    owner = dest_flat * ocean_blocks + dest_block.reshape(pair_count)
    adjoint = adjoint_of(
        owner, gathered.reshape(space_size * ocean_blocks, channels, cells), remap_tiles
    )
    hidden, outputs = w_out.shape
    grad_in = summed[:, :, :hidden].reshape(channels, hidden)
    grad_out = summed[: hidden // 128, :outputs, hidden:]
    return (adjoint[None], grad_in, grad_out.transpose(0, 2, 1).reshape(hidden, outputs))


def solution(mesh):
    body = fused_body if mesh.shape["level"] == 1 and mesh.shape["space"] in (6, 8) else general_body
    return jax.shard_map(
        body,
        mesh=mesh,
        in_specs=(
            P("member", ("group", "space"), None, None),
            P("space", None, None, None),
            P("space", None),
            P("space", None),
            P("space", None),
            P("member", ("group", "space"), None, None),
            P(None, "level"),
            P("level", None),
        ),
        out_specs=(
            P("member", ("group", "space"), "level", None),
            P("group", "level"),
            P("level", "group"),
        ),
        check_vma=False,
    )
```

```python
import math

import jax
import jax.numpy as jnp
from jax import lax
from jax.experimental import pallas as pl
from jax.experimental.pallas import tpu as pltpu
from jax.sharding import PartitionSpec as P


def remap_pieces(source, remap_tiles, slot_index, slot_total):
    pieces = jnp.einsum(
        "aci,akij->akcj", source, remap_tiles, preferred_element_type=jnp.float32
    ).astype(jnp.bfloat16)
    pair_count = pieces.shape[0] * pieces.shape[1]
    pieces = pieces.reshape(pair_count, source.shape[1], source.shape[2])
    return (
        jnp.zeros((slot_total, source.shape[1], source.shape[2]), jnp.bfloat16)
        .at[slot_index]
        .set(pieces)
    )


def add_pieces(received, received_ids, ocean_blocks):
    flat_data = received.reshape(-1, received.shape[2], received.shape[3]).astype(jnp.float32)
    summed = jnp.zeros((ocean_blocks + 1, received.shape[2], received.shape[3]), jnp.float32)
    summed = summed.at[received_ids.reshape(-1)].add(flat_data)
    return summed[:ocean_blocks].astype(jnp.bfloat16)


def general_body(atm_state, remap_tiles, dest_device, dest_block, wet_mask, target, w_in, w_out):
    space_size = lax.axis_size("space")
    member_size = lax.axis_size("member")
    level_size = lax.axis_size("level")
    atm_blocks, top_count, cells, _ = remap_tiles.shape
    ocean_blocks = wet_mask.shape[0]
    channels = atm_state.shape[2]
    half_chan = channels // level_size
    capacity = min(atm_blocks, max(2, 2 * atm_blocks * top_count // space_size))
    pair_count = atm_blocks * top_count
    slot_total = space_size * capacity
    dest_flat = dest_device.reshape(pair_count)
    onehot = (dest_flat[:, None] == jnp.arange(space_size, dtype=jnp.int32)[None, :]).astype(
        jnp.int32
    )
    slot_rank = jnp.sum((jnp.cumsum(onehot, axis=0) - onehot) * onehot, axis=1)
    slot_index = dest_flat * capacity + slot_rank
    send_ids = (
        jnp.full((slot_total,), ocean_blocks, jnp.int32)
        .at[slot_index]
        .set(dest_block.reshape(pair_count))
    )
    send_ids = send_ids.reshape(space_size, capacity)
    local_state = atm_state[0]
    outgoing = remap_pieces(local_state, remap_tiles, slot_index, slot_total).reshape(
        space_size, capacity, channels, cells
    )
    received, received_ids = (
        lax.all_to_all(outgoing, "space", split_axis=0, concat_axis=0, tiled=True),
        lax.all_to_all(send_ids, "space", split_axis=0, concat_axis=0, tiled=True),
    )
    features = add_pieces(received, received_ids, ocean_blocks)
    pre_act = jnp.einsum("ch,ocj->ohj", w_in, features, preferred_element_type=jnp.float32)
    activated = jax.nn.silu(pre_act).astype(jnp.bfloat16)
    partial_flux = jnp.einsum("hq,ohj->oqj", w_out, activated, preferred_element_type=jnp.float32)
    predicted = lax.psum(partial_flux, "level")
    misfit = wet_mask.astype(jnp.float32)[:, None, :] * (predicted - target[0])
    act_grad = jnp.einsum(
        "hq,oqj->ohj", w_out.astype(jnp.float32), misfit, precision=lax.Precision.HIGHEST
    )
    gate_value = jax.nn.sigmoid(pre_act)
    pre_grad = (act_grad * gate_value * (1.0 + pre_act * (1.0 - gate_value))).astype(jnp.bfloat16)
    feat_grad = lax.psum_scatter(
        jnp.einsum("ch,ohj->coj", w_in, pre_grad, preferred_element_type=jnp.float32),
        "level",
        scatter_dimension=0,
        tiled=True,
    ).astype(jnp.bfloat16)
    reply = jnp.take(feat_grad, received_ids.reshape(-1), axis=1, mode="clip")
    reply = reply.reshape(half_chan, space_size, capacity, cells)
    returned = lax.all_to_all(reply, "space", split_axis=1, concat_axis=1, tiled=True)
    pair_grad = jnp.take(returned.reshape(half_chan, slot_total, cells), slot_index, axis=1)
    pair_grad = pair_grad.reshape(half_chan, atm_blocks, top_count, cells)
    adjoint = jnp.einsum(
        "cakj,akij->aci", pair_grad, remap_tiles, preferred_element_type=jnp.float32
    )
    cell_total = member_size * space_size * ocean_blocks * cells
    scale_in = math.sqrt(w_in.shape[1] * level_size / cell_total)
    scale_out = 1.0 / math.sqrt(cell_total)
    grad_in = scale_in * jnp.einsum(
        "ocj,ohj->ch", features, pre_grad, preferred_element_type=jnp.float32
    )
    grad_out = scale_out * jnp.einsum(
        "ohj,oqj->hq",
        activated,
        misfit,
        preferred_element_type=jnp.float32,
        precision=lax.Precision.HIGHEST,
    )
    grad_in, grad_out = lax.psum((grad_in, grad_out), ("space", "member"))
    return (adjoint[None], grad_in, grad_out)


VMEM_BYTES = 48 * 1024 * 1024


def slots_kernel(pair_ref, tiles_ref, out_ref):
    @pl.loop(0, out_ref.shape[0], unroll=4)
    def _(slot):
        out_ref[slot] = tiles_ref[pair_ref[slot]]


def slotted_tiles(pairs, tiles):
    whole = pl.BlockSpec(memory_space=pltpu.VMEM)
    return pl.pallas_call(
        slots_kernel,
        out_shape=jax.ShapeDtypeStruct(pairs.shape + tiles.shape[1:], tiles.dtype),
        in_specs=[pl.BlockSpec(memory_space=pltpu.SMEM), whole],
        out_specs=whole,
        compiler_params=pltpu.CompilerParams(vmem_limit_bytes=VMEM_BYTES),
    )(pairs, tiles)


def adjoint_kernel(slot_ref, back_ref, tiles_ref, out_ref):
    step = pl.program_id(0)
    blocks, top_count = tiles_ref.shape[:2]
    for a in range(blocks):
        first = (step * blocks + a) * top_count
        grads = jnp.concatenate([back_ref[slot_ref[first + k]] for k in range(top_count)], axis=1)
        wide = jnp.concatenate([tiles_ref[a, k] for k in range(top_count)], axis=1)
        out_ref[a] = lax.dot_general(
            grads, wide, (((1,), (1,)), ((), ())), preferred_element_type=jnp.float32
        )


def adjoint_of(slot_index, returned, tiles):
    atm_blocks, top_count, cells, _ = tiles.shape
    slots, channels, _ = returned.shape
    per_step = math.gcd(atm_blocks, 4)
    return pl.pallas_call(
        adjoint_kernel,
        out_shape=jax.ShapeDtypeStruct((atm_blocks, channels, cells), jnp.float32),
        grid_spec=pltpu.PrefetchScalarGridSpec(
            num_scalar_prefetch=1,
            grid=(atm_blocks // per_step,),
            in_specs=[
                pl.BlockSpec((slots, channels, cells), lambda s, _: (0, 0, 0)),
                pl.BlockSpec((per_step, top_count, cells, cells), lambda s, _: (s, 0, 0, 0)),
            ],
            out_specs=pl.BlockSpec((per_step, channels, cells), lambda s, _: (s, 0, 0)),
        ),
        compiler_params=pltpu.CompilerParams(vmem_limit_bytes=VMEM_BYTES),
    )(slot_index, returned, tiles)


def features_kernel(id_ref, state_at_ref, states_ref, slots_ref, feat_ref, total_ref):
    slots = slots_ref.shape[0]
    total_ref[...] = jnp.zeros_like(total_ref)
    batch = math.gcd(slots, 8)

    @pl.loop(0, slots // batch)
    def _(step):
        places = [step * batch + b for b in range(batch)]
        pieces = [
            jnp.dot(
                states_ref[state_at_ref[slot]], slots_ref[slot], preferred_element_type=jnp.float32
            ).astype(jnp.bfloat16)
            for slot in places
        ]
        for slot, piece in zip(places, pieces):
            total_ref[id_ref[slot]] += piece.astype(jnp.float32)

    feat_ref[...] = total_ref[0 : feat_ref.shape[0]].astype(jnp.bfloat16)


def features_of(states, tiles, state_at, ids, ocean_blocks):
    _, channels, cells = states.shape
    whole = pl.BlockSpec(memory_space=pltpu.VMEM)
    return pl.pallas_call(
        features_kernel,
        out_shape=jax.ShapeDtypeStruct((ocean_blocks, channels, cells), jnp.bfloat16),
        in_specs=[pl.BlockSpec(memory_space=pltpu.SMEM)] * 2 + [whole] * 2,
        out_specs=whole,
        scratch_shapes=[pltpu.VMEM((ocean_blocks + 1, channels, cells), jnp.float32)],
        compiler_params=pltpu.CompilerParams(vmem_limit_bytes=VMEM_BYTES),
    )(ids, state_at, states, tiles)


PARTS = 4
CHUNKS = 2
MESH = pl.DeviceIdType.MESH


def exchange_kernel(
    space_size,
    member_size,
    scale_in,
    scale_out,
    features_ref,
    mask_ref,
    goal_ref,
    w_in_ref,
    w_in_t_ref,
    w_out_t_ref,
    w_out_3_ref,
    all_ref,
    sums_ref,
    feat_ref,
    grads_ref,
    in_ref,
    pre_ref,
    act_ref,
    out_ref,
    team_box,
    partial,
    place_box,
    total,
    team_send,
    team_recv,
    place_send,
    place_recv,
    line_send,
    line_recv,
    pair_send,
    pair_recv,
    own_sem,
):
    space, member = lax.axis_index("space"), lax.axis_index("member")
    length = space_size // 2
    place, core = space // 2, space % 2
    size = feat_ref.shape[0] // PARTS

    teams = 2 * member_size
    team = member * 2 + core

    def mate(i):
        other = lax.rem(team + i, teams)
        return other, {"space": place * 2 + other % 2, "member": other // 2}

    def far(i):
        other = lax.rem(place + i, length)
        return other, {"space": other * 2 + core}

    barrier = pltpu.get_barrier_semaphore()
    for i in range(1, teams):
        pl.semaphore_signal(barrier, inc=1, device_id=mate(i)[1], device_id_type=MESH)
    for i in range(1, length):
        pl.semaphore_signal(barrier, inc=1, device_id=far(i)[1], device_id_type=MESH)
    pl.semaphore_wait(barrier, teams + length - 2)

    def team_copy(back, i, owner):
        other, device = mate(i)
        rows = pl.ds((owner if back else other) * length, length)
        return pltpu.make_async_remote_copy(
            src_ref=sums_ref.at[rows] if back else grads_ref.at[rows],
            dst_ref=sums_ref.at[rows] if back else team_box.at[i - 1],
            send_sem=team_send.at[back, i - 1],
            recv_sem=team_recv.at[back, i - 1],
            device_id=device,
            device_id_type=MESH,
        )

    def place_copy(back, i, owner):
        other, device = far(i)
        return pltpu.make_async_remote_copy(
            src_ref=total if back else partial.at[other],
            dst_ref=sums_ref.at[team * length + owner] if back else place_box.at[i - 1],
            send_sem=place_send.at[back, i - 1],
            recv_sem=place_recv.at[back, i - 1],
            device_id=device,
            device_id_type=MESH,
        )

    own_sum = pltpu.make_async_copy(total, sums_ref.at[team * length + place], own_sem.at[1])

    def sum_team():
        for i in range(1, teams):
            team_copy(0, i, team).wait_recv()
        value = grads_ref[pl.ds(team * length, length)]
        for i in range(1, teams):
            value += team_box[i - 1]
        partial[...] = value
        for i in range(1, length):
            place_copy(0, i, place).start()

    def sum_places():
        for i in range(1, length):
            place_copy(0, i, place).wait_recv()
        value = partial[place]
        for i in range(1, length):
            value += place_box[i - 1]
        total[...] = value
        for i in range(1, length):
            place_copy(1, i, place).start()
        own_sum.start()

    def share_sums():
        for i in range(1, length):
            place_copy(1, i, far(length - i)[0]).wait_recv()
        own_sum.wait()
        for i in range(1, teams):
            team_copy(1, i, team).start()

    phases = [sum_team, sum_places, share_sums]

    def source(origin, own, c):
        rows = pl.ds(c * size, size)
        return feat_ref.at[rows] if own else all_ref.at[origin, rows]

    def line(way, hop, c, origin, own):
        step = 1 if way == 0 else -1
        return pltpu.make_async_remote_copy(
            src_ref=source(origin, own, c),
            dst_ref=all_ref.at[origin, pl.ds(c * size, size)],
            send_sem=line_send.at[way, hop, c],
            recv_sem=line_recv.at[way, hop, c],
            device_id={"space": (place + step) * 2 + core},
            device_id_type=MESH,
        )

    def pair(index, c, origin, own):
        return pltpu.make_async_remote_copy(
            src_ref=source(origin, own, c),
            dst_ref=all_ref.at[origin, pl.ds(c * size, size)],
            send_sem=pair_send.at[index, c],
            recv_sem=pair_recv.at[index, c],
            device_id={"space": place * 2 + 1 - core},
            device_id_type=MESH,
        )

    def behind(way, hop):
        at = place - 1 - hop if way == 0 else place + 1 + hop
        return at, (at >= 0 if way == 0 else at < length)

    ahead = (place < length - 1, place > 0)
    own_copy = pltpu.make_async_copy(feat_ref, all_ref.at[space], own_sem.at[0])
    hidden, channels = w_in_t_ref.shape
    cells = feat_ref.shape[2]
    group = math.gcd(size, 4)
    chunk = math.gcd(hidden, 256)
    in_ref[...] = jnp.zeros_like(in_ref)
    out_ref[...] = jnp.zeros_like(out_ref)

    @pl.loop(0, PARTS)
    def _(c):
        @pl.loop(c * (size // group), (c + 1) * (size // group))
        def _(step):
            first = step * group
            feat = jnp.concatenate(
                [features_ref[first + g] for g in range(group)], axis=1
            )
            predicted = jnp.zeros((8, group * cells), jnp.float32)
            for h in range(0, hidden, chunk):
                rows = slice(h, h + chunk)
                pre = jnp.dot(w_in_t_ref[rows], feat, preferred_element_type=jnp.float32)
                pre_ref[rows] = pre
                act = (pre * jax.nn.sigmoid(pre)).astype(jnp.bfloat16)
                act_ref[rows] = act
                predicted += jnp.dot(w_out_t_ref[:, rows], act, preferred_element_type=jnp.float32)
            goal = jnp.concatenate([goal_ref[first + g] for g in range(group)], axis=1)
            mask = jnp.concatenate([mask_ref[first + g] for g in range(group)], axis=1)
            misfit = mask * (predicted - goal)
            high = misfit.astype(jnp.bfloat16).astype(jnp.float32)
            rest = misfit - high
            middle = rest.astype(jnp.bfloat16).astype(jnp.float32)
            low = rest - middle
            misfit_3 = jnp.concatenate([high, middle, low, jnp.zeros_like(low)], axis=0).astype(
                jnp.bfloat16
            )
            feat_grad = jnp.zeros((channels, group * cells), jnp.float32)
            for h in range(0, hidden, chunk):
                rows = slice(h, h + chunk)
                act_grad = jnp.dot(w_out_3_ref[rows], misfit_3, preferred_element_type=jnp.float32)
                pre = pre_ref[rows]
                gate = jax.nn.sigmoid(pre)
                pre_grad = (act_grad * gate * (1.0 + pre * (1.0 - gate))).astype(jnp.bfloat16)
                feat_grad += jnp.dot(w_in_ref[:, rows], pre_grad, preferred_element_type=jnp.float32)
                in_ref[:, rows] += lax.dot_general(
                    feat, pre_grad, (((1,), (1,)), ((), ())), preferred_element_type=jnp.float32
                )
                out_ref[:, rows] += lax.dot_general(
                    misfit_3, act_ref[rows], (((1,), (1,)), ((), ())), preferred_element_type=jnp.float32
                )
            for g in range(group):
                feat_ref[first + g] = feat_grad[:, g * cells : (g + 1) * cells].astype(jnp.bfloat16)

        for way in range(2):

            @pl.when(ahead[way])
            def _():
                line(way, 0, c, space, True).start()

        pair(0, c, space, True).start()

    out = scale_out * (out_ref[0:8] + out_ref[8:16] + out_ref[16:24])
    for p in range(grads_ref.shape[0]):
        grads_ref[p, :, 0:hidden] = scale_in * in_ref[8 * p : 8 * p + 8]
        if (p + 1) * 128 <= hidden:
            grads_ref[p, :, hidden : hidden + 128] = out[:, p * 128 : (p + 1) * 128]
        else:
            grads_ref[p, :, hidden : hidden + 128] = jnp.zeros((8, 128), jnp.float32)

    for i in range(1, teams):
        team_copy(0, i, team).start()
    own_copy.start()

    for hop in range(length - 1):
        for c in range(PARTS):
            for way in range(2):
                at, there = behind(way, hop)
                origin = at * 2 + core

                @pl.when(there)
                def _():
                    line(way, hop, c, origin, False).wait_recv()
                    if hop + 1 < length - 1:

                        @pl.when(ahead[way])
                        def _():
                            line(way, hop + 1, c, origin, False).start()

                    pair(1 + way * (length - 1) + hop, c, origin, False).start()

            if phases:
                phases.pop(0)()

    own_copy.wait()
    for back in range(2):
        for i in range(1, teams):
            team_copy(back, i, team).wait_send()
        for i in range(1, length):
            place_copy(back, i, place).wait_send()
    for i in range(1, teams):
        team_copy(1, i, mate(teams - i)[0]).wait_recv()
    for c in range(PARTS):
        pair(0, c, space, True).wait_send()
        pair(0, c, place * 2 + 1 - core, False).wait_recv()
        for way in range(2):

            @pl.when(ahead[way])
            def _():
                line(way, 0, c, space, True).wait_send()

            for hop in range(length - 1):
                at, there = behind(way, hop)
                origin = at * 2 + core
                index = 1 + way * (length - 1) + hop

                @pl.when(there)
                def _():
                    if hop + 1 < length - 1:

                        @pl.when(ahead[way])
                        def _():
                            line(way, hop + 1, c, origin, False).wait_send()

                    pair(index, c, origin, False).wait_send()
                    pair(index, c, at * 2 + 1 - core, False).wait_recv()


def exchange(
    features, wet_mask, target, w_in, w_out, scale_in, scale_out, space_size, member_size
):
    ocean_blocks, channels, cells = features.shape
    hidden, outputs = w_out.shape
    group = math.gcd(ocean_blocks // PARTS, 4)
    padded = jnp.pad(w_out, ((0, 0), (0, 8 - outputs)))
    teams, length = 2 * member_size, space_size // 2
    hops = length - 1
    piece = (8, hidden + 128)
    dma = pltpu.SemaphoreType.DMA
    anywhere = pl.BlockSpec(memory_space=pl.ANY)
    return pl.pallas_call(
        lambda *refs: exchange_kernel(space_size, member_size, scale_in, scale_out, *refs),
        out_shape=(
            jax.ShapeDtypeStruct((space_size,) + features.shape, features.dtype),
            jax.ShapeDtypeStruct((channels // 8,) + piece, jnp.float32),
        ),
        in_specs=[pl.BlockSpec(memory_space=pltpu.VMEM)] * 7,
        out_specs=(anywhere, anywhere),
        scratch_shapes=[
            pltpu.VMEM(features.shape, features.dtype),
            pltpu.VMEM((channels // 8,) + piece, jnp.float32),
            pltpu.VMEM((channels, hidden), jnp.float32),
            pltpu.VMEM((hidden, group * cells), jnp.float32),
            pltpu.VMEM((hidden, group * cells), jnp.bfloat16),
            pltpu.VMEM((32, hidden), jnp.float32),
            pltpu.VMEM((teams - 1, length) + piece, jnp.float32),
            pltpu.VMEM((length,) + piece, jnp.float32),
            pltpu.VMEM((length - 1,) + piece, jnp.float32),
            pltpu.VMEM(piece, jnp.float32),
            dma((2, teams - 1)),
            dma((2, teams - 1)),
            dma((2, length - 1)),
            dma((2, length - 1)),
            dma((2, hops, PARTS)),
            dma((2, hops, PARTS)),
            dma((1 + 2 * hops, PARTS)),
            dma((1 + 2 * hops, PARTS)),
            dma((2,)),
        ],
        compiler_params=pltpu.CompilerParams(
            collective_id=0, has_side_effects=True, vmem_limit_bytes=VMEM_BYTES
        ),
    )(
        features,
        wet_mask.astype(jnp.float32)[:, None, :],
        jnp.pad(target, ((0, 0), (0, 8 - outputs), (0, 0))),
        w_in,
        w_in.T,
        padded.T,
        jnp.concatenate([padded, padded, padded, jnp.zeros_like(padded)], axis=1),
    )


def spread_kernel(
    space_size,
    columns,
    member_size,
    state_ref,
    tiles_ref,
    codes_ref,
    states_ref,
    slots_ref,
    all_codes_ref,
    code_send,
    code_recv,
    tile_send,
    tile_recv,
    share_send,
    share_recv,
    line_send,
    line_recv,
    pair_send,
    pair_recv,
    own_sem,
):
    group, space, member = (lax.axis_index(name) for name in ("group", "space", "member"))
    column = group * member_size + member
    length = space_size // 2
    place, core = space // 2, space % 2
    size = state_ref.shape[0] // CHUNKS
    share = tiles_ref.shape[1]

    def along(j):
        return lax.rem(space + j, space_size)

    def across(i):
        other = lax.rem(column + i, columns)
        return other, {"group": other // member_size, "member": other % member_size}

    barrier = pltpu.get_barrier_semaphore()
    for j in range(1, space_size):
        pl.semaphore_signal(barrier, inc=1, device_id={"space": along(j)}, device_id_type=MESH)
    for i in range(1, columns):
        pl.semaphore_signal(barrier, inc=1, device_id=across(i)[1], device_id_type=MESH)
    pl.semaphore_wait(barrier, space_size + columns - 2)

    def part(origin, owner):
        return slots_ref.at[origin, pl.ds(owner * share, share)]

    def tile(j, origin):
        return pltpu.make_async_remote_copy(
            src_ref=tiles_ref.at[along(j)],
            dst_ref=part(origin, column),
            send_sem=tile_send.at[j - 1],
            recv_sem=tile_recv.at[j - 1],
            device_id={"space": along(j)},
            device_id_type=MESH,
        )

    def code(j, origin):
        return pltpu.make_async_remote_copy(
            src_ref=codes_ref.at[along(j)],
            dst_ref=all_codes_ref.at[origin],
            send_sem=code_send.at[j - 1],
            recv_sem=code_recv.at[j - 1],
            device_id={"space": along(j)},
            device_id_type=MESH,
        )

    def shared(i, j, owner):
        origin = along(space_size - j)
        return pltpu.make_async_remote_copy(
            src_ref=tiles_ref.at[space] if j == 0 else part(origin, column),
            dst_ref=part(origin, owner),
            send_sem=share_send.at[i - 1, j],
            recv_sem=share_recv.at[i - 1, j],
            device_id=across(i)[1],
            device_id_type=MESH,
        )

    def source(origin, own, c):
        rows = pl.ds(c * size, size)
        return state_ref.at[rows] if own else states_ref.at[origin, rows]

    def line(way, hop, c, origin, own):
        step = 1 if way == 0 else -1
        return pltpu.make_async_remote_copy(
            src_ref=source(origin, own, c),
            dst_ref=states_ref.at[origin, pl.ds(c * size, size)],
            send_sem=line_send.at[way, hop, c],
            recv_sem=line_recv.at[way, hop, c],
            device_id={"space": (place + step) * 2 + core},
            device_id_type=MESH,
        )

    def pair(index, c, origin, own):
        return pltpu.make_async_remote_copy(
            src_ref=source(origin, own, c),
            dst_ref=states_ref.at[origin, pl.ds(c * size, size)],
            send_sem=pair_send.at[index, c],
            recv_sem=pair_recv.at[index, c],
            device_id={"space": place * 2 + 1 - core},
            device_id_type=MESH,
        )

    def behind(way, hop):
        at = place - 1 - hop if way == 0 else place + 1 + hop
        return at, (at >= 0 if way == 0 else at < length)

    ahead = (place < length - 1, place > 0)
    for j in range(1, space_size):
        code(j, space).start()
        tile(j, space).start()
    own_codes = pltpu.make_async_copy(codes_ref.at[space], all_codes_ref.at[space], own_sem.at[2])
    own_codes.start()
    own_state = pltpu.make_async_copy(state_ref, states_ref.at[space], own_sem.at[0])
    own_tiles = pltpu.make_async_copy(tiles_ref.at[space], part(space, column), own_sem.at[1])
    for i in range(1, columns):
        shared(i, 0, column).start()
    for c in range(CHUNKS):
        for way in range(2):

            @pl.when(ahead[way])
            def _():
                line(way, 0, c, space, True).start()

        pair(0, c, space, True).start()
    own_state.start()
    own_tiles.start()

    order = list(range(1, space_size))
    hops = length - 1
    for hop in range(hops):
        for j in order[hop * len(order) // hops : (hop + 1) * len(order) // hops]:
            tile(j, along(space_size - j)).wait_recv()
            for i in range(1, columns):
                shared(i, j, column).start()
        for c in range(CHUNKS):
            for way in range(2):
                at, there = behind(way, hop)
                origin = at * 2 + core

                @pl.when(there)
                def _():
                    line(way, hop, c, origin, False).wait_recv()
                    if hop + 1 < hops:

                        @pl.when(ahead[way])
                        def _():
                            line(way, hop + 1, c, origin, False).start()

                    pair(1 + way * hops + hop, c, origin, False).start()

    own_state.wait()
    own_tiles.wait()
    own_codes.wait()
    for j in range(1, space_size):
        code(j, along(space_size - j)).wait_recv()
        code(j, space).wait_send()
        tile(j, space).wait_send()
    for i in range(1, columns):
        for j in range(space_size):
            shared(i, j, across(columns - i)[0]).wait_recv()
            shared(i, j, column).wait_send()
    for c in range(CHUNKS):
        pair(0, c, space, True).wait_send()
        pair(0, c, place * 2 + 1 - core, False).wait_recv()
        for way in range(2):

            @pl.when(ahead[way])
            def _():
                line(way, 0, c, space, True).wait_send()

            for hop in range(hops):
                at, there = behind(way, hop)
                origin = at * 2 + core
                index = 1 + way * hops + hop

                @pl.when(there)
                def _():
                    if hop + 1 < hops:

                        @pl.when(ahead[way])
                        def _():
                            line(way, hop + 1, c, origin, False).wait_send()

                    pair(index, c, origin, False).wait_send()
                    pair(index, c, at * 2 + 1 - core, False).wait_recv()


def spread(state, tile_slots, codes, space_size, columns, member_size):
    hops = space_size // 2 - 1
    _, share, cells, _ = tile_slots.shape
    dma = pltpu.SemaphoreType.DMA
    anywhere = pl.BlockSpec(memory_space=pl.ANY)
    return pl.pallas_call(
        lambda *refs: spread_kernel(space_size, columns, member_size, *refs),
        out_shape=(
            jax.ShapeDtypeStruct((space_size,) + state.shape, state.dtype),
            jax.ShapeDtypeStruct((space_size, columns * share, cells, cells), tile_slots.dtype),
            jax.ShapeDtypeStruct(codes.shape, codes.dtype),
        ),
        in_specs=[anywhere] * 3,
        out_specs=(anywhere,) * 3,
        scratch_shapes=[
            dma((space_size - 1,)),
            dma((space_size - 1,)),
            dma((space_size - 1,)),
            dma((space_size - 1,)),
            dma((columns - 1, space_size)),
            dma((columns - 1, space_size)),
            dma((2, hops, CHUNKS)),
            dma((2, hops, CHUNKS)),
            dma((1 + 2 * hops, CHUNKS)),
            dma((1 + 2 * hops, CHUNKS)),
            dma((3,)),
        ],
        compiler_params=pltpu.CompilerParams(
            collective_id=1, has_side_effects=True, vmem_limit_bytes=VMEM_BYTES
        ),
    )(state, tile_slots, codes)


def fused_body(atm_state, remap_tiles, dest_device, dest_block, wet_mask, target, w_in, w_out):
    space_size = lax.axis_size("space")
    member_size = lax.axis_size("member")
    atm_blocks, top_count, cells, _ = remap_tiles.shape
    ocean_blocks = wet_mask.shape[0]
    channels = atm_state.shape[2]
    pieces_fit = channels == 8 * space_size * member_size and w_in.shape[1] <= 16 * channels
    columns = lax.axis_size("group") * member_size
    capacity = min(atm_blocks, max(2, 2 * atm_blocks * top_count // space_size))
    if not pieces_fit or ocean_blocks % PARTS or atm_blocks % CHUNKS or capacity % columns:
        return general_body(
            atm_state, remap_tiles, dest_device, dest_block, wet_mask, target, w_in, w_out
        )
    pair_count = atm_blocks * top_count
    slot_total = space_size * capacity
    dest_flat = dest_device.reshape(pair_count)
    onehot = (dest_flat[:, None] == jnp.arange(space_size, dtype=jnp.int32)[None, :]).astype(
        jnp.int32
    )
    slot_rank = jnp.sum((jnp.cumsum(onehot, axis=0) - onehot) * onehot, axis=1)
    slot_index = dest_flat * capacity + slot_rank
    codes = (
        jnp.full((slot_total,), ocean_blocks * pair_count, jnp.int32)
        .at[slot_index]
        .set(dest_block.reshape(pair_count) * pair_count + jnp.arange(pair_count, dtype=jnp.int32))
    ).reshape(space_size, capacity)
    share = capacity // columns
    column = lax.axis_index("group") * member_size + lax.axis_index("member")
    mine = lax.dynamic_slice_in_dim(codes, column * share, share, axis=1)
    tile_slots = slotted_tiles(
        (mine % pair_count).reshape(-1), remap_tiles.reshape(pair_count, cells, cells)
    ).reshape(space_size, share, cells, cells)
    wide_codes = jnp.broadcast_to(
        jnp.pad(codes, ((0, 0), (0, -capacity % 128)))[:, None, :], (space_size, 8, -(-capacity // 128) * 128)
    )
    states, tiles, received_codes = spread(
        atm_state[0], tile_slots, wide_codes, space_size, columns, member_size
    )
    received_codes = received_codes[:, 0, :capacity]
    received_ids = (received_codes // pair_count).reshape(slot_total)
    state_at = (
        jnp.arange(space_size, dtype=jnp.int32)[:, None] * atm_blocks
        + received_codes % pair_count // top_count
    ).reshape(slot_total)
    cell_total = member_size * space_size * ocean_blocks * cells
    scale_in = math.sqrt(w_in.shape[1] / cell_total)
    scale_out = 1.0 / math.sqrt(cell_total)
    features = features_of(
        states.reshape(space_size * atm_blocks, channels, cells),
        tiles.reshape(slot_total, cells, cells),
        state_at,
        received_ids,
        ocean_blocks,
    )
    gathered, summed = exchange(
        features, wet_mask, target[0], w_in, w_out, scale_in, scale_out, space_size, member_size
    )
    owner = dest_flat * ocean_blocks + dest_block.reshape(pair_count)
    adjoint = adjoint_of(
        owner, gathered.reshape(space_size * ocean_blocks, channels, cells), remap_tiles
    )
    hidden, outputs = w_out.shape
    grad_in = summed[:, :, :hidden].reshape(channels, hidden)
    grad_out = summed[: hidden // 128, :outputs, hidden:]
    return (adjoint[None], grad_in, grad_out.transpose(0, 2, 1).reshape(hidden, outputs))


def solution(mesh):
    body = fused_body if mesh.shape["level"] == 1 and mesh.shape["space"] in (6, 8) else general_body
    return jax.shard_map(
        body,
        mesh=mesh,
        in_specs=(
            P("member", ("group", "space"), None, None),
            P("space", None, None, None),
            P("space", None),
            P("space", None),
            P("space", None),
            P("member", ("group", "space"), None, None),
            P(None, "level"),
            P("level", None),
        ),
        out_specs=(
            P("member", ("group", "space"), "level", None),
            P("group", "level"),
            P("level", "group"),
        ),
        check_vma=False,
    )
```

```python
import math

import jax
import jax.numpy as jnp
from jax import lax
from jax.experimental import pallas as pl
from jax.experimental.pallas import tpu as pltpu
from jax.sharding import PartitionSpec as P


def remap_pieces(source, remap_tiles, slot_index, slot_total):
    pieces = jnp.einsum(
        "aci,akij->akcj", source, remap_tiles, preferred_element_type=jnp.float32
    ).astype(jnp.bfloat16)
    pair_count = pieces.shape[0] * pieces.shape[1]
    pieces = pieces.reshape(pair_count, source.shape[1], source.shape[2])
    return (
        jnp.zeros((slot_total, source.shape[1], source.shape[2]), jnp.bfloat16)
        .at[slot_index]
        .set(pieces)
    )


def add_pieces(received, received_ids, ocean_blocks):
    flat_data = received.reshape(-1, received.shape[2], received.shape[3]).astype(jnp.float32)
    summed = jnp.zeros((ocean_blocks + 1, received.shape[2], received.shape[3]), jnp.float32)
    summed = summed.at[received_ids.reshape(-1)].add(flat_data)
    return summed[:ocean_blocks].astype(jnp.bfloat16)


def general_body(atm_state, remap_tiles, dest_device, dest_block, wet_mask, target, w_in, w_out):
    space_size = lax.axis_size("space")
    member_size = lax.axis_size("member")
    level_size = lax.axis_size("level")
    atm_blocks, top_count, cells, _ = remap_tiles.shape
    ocean_blocks = wet_mask.shape[0]
    channels = atm_state.shape[2]
    half_chan = channels // level_size
    capacity = min(atm_blocks, max(2, 2 * atm_blocks * top_count // space_size))
    pair_count = atm_blocks * top_count
    slot_total = space_size * capacity
    dest_flat = dest_device.reshape(pair_count)
    onehot = (dest_flat[:, None] == jnp.arange(space_size, dtype=jnp.int32)[None, :]).astype(
        jnp.int32
    )
    slot_rank = jnp.sum((jnp.cumsum(onehot, axis=0) - onehot) * onehot, axis=1)
    slot_index = dest_flat * capacity + slot_rank
    send_ids = (
        jnp.full((slot_total,), ocean_blocks, jnp.int32)
        .at[slot_index]
        .set(dest_block.reshape(pair_count))
    )
    send_ids = send_ids.reshape(space_size, capacity)
    local_state = atm_state[0]
    outgoing = remap_pieces(local_state, remap_tiles, slot_index, slot_total).reshape(
        space_size, capacity, channels, cells
    )
    received, received_ids = (
        lax.all_to_all(outgoing, "space", split_axis=0, concat_axis=0, tiled=True),
        lax.all_to_all(send_ids, "space", split_axis=0, concat_axis=0, tiled=True),
    )
    features = add_pieces(received, received_ids, ocean_blocks)
    pre_act = jnp.einsum("ch,ocj->ohj", w_in, features, preferred_element_type=jnp.float32)
    activated = jax.nn.silu(pre_act).astype(jnp.bfloat16)
    partial_flux = jnp.einsum("hq,ohj->oqj", w_out, activated, preferred_element_type=jnp.float32)
    predicted = lax.psum(partial_flux, "level")
    misfit = wet_mask.astype(jnp.float32)[:, None, :] * (predicted - target[0])
    act_grad = jnp.einsum(
        "hq,oqj->ohj", w_out.astype(jnp.float32), misfit, precision=lax.Precision.HIGHEST
    )
    gate_value = jax.nn.sigmoid(pre_act)
    pre_grad = (act_grad * gate_value * (1.0 + pre_act * (1.0 - gate_value))).astype(jnp.bfloat16)
    feat_grad = lax.psum_scatter(
        jnp.einsum("ch,ohj->coj", w_in, pre_grad, preferred_element_type=jnp.float32),
        "level",
        scatter_dimension=0,
        tiled=True,
    ).astype(jnp.bfloat16)
    reply = jnp.take(feat_grad, received_ids.reshape(-1), axis=1, mode="clip")
    reply = reply.reshape(half_chan, space_size, capacity, cells)
    returned = lax.all_to_all(reply, "space", split_axis=1, concat_axis=1, tiled=True)
    pair_grad = jnp.take(returned.reshape(half_chan, slot_total, cells), slot_index, axis=1)
    pair_grad = pair_grad.reshape(half_chan, atm_blocks, top_count, cells)
    adjoint = jnp.einsum(
        "cakj,akij->aci", pair_grad, remap_tiles, preferred_element_type=jnp.float32
    )
    cell_total = member_size * space_size * ocean_blocks * cells
    scale_in = math.sqrt(w_in.shape[1] * level_size / cell_total)
    scale_out = 1.0 / math.sqrt(cell_total)
    grad_in = scale_in * jnp.einsum(
        "ocj,ohj->ch", features, pre_grad, preferred_element_type=jnp.float32
    )
    grad_out = scale_out * jnp.einsum(
        "ohj,oqj->hq",
        activated,
        misfit,
        preferred_element_type=jnp.float32,
        precision=lax.Precision.HIGHEST,
    )
    grad_in, grad_out = lax.psum((grad_in, grad_out), ("space", "member"))
    return (adjoint[None], grad_in, grad_out)


VMEM_BYTES = 48 * 1024 * 1024


def slots_kernel(pair_ref, tiles_ref, out_ref):
    @pl.loop(0, out_ref.shape[0], unroll=4)
    def _(slot):
        out_ref[slot] = tiles_ref[pair_ref[slot]]


def slotted_tiles(pairs, tiles):
    whole = pl.BlockSpec(memory_space=pltpu.VMEM)
    return pl.pallas_call(
        slots_kernel,
        out_shape=jax.ShapeDtypeStruct(pairs.shape + tiles.shape[1:], tiles.dtype),
        in_specs=[pl.BlockSpec(memory_space=pltpu.SMEM), whole],
        out_specs=whole,
        compiler_params=pltpu.CompilerParams(vmem_limit_bytes=VMEM_BYTES),
    )(pairs, tiles)


def adjoint_kernel(slot_ref, back_ref, tiles_ref, out_ref):
    step = pl.program_id(0)
    blocks, top_count = tiles_ref.shape[:2]
    for a in range(blocks):
        first = (step * blocks + a) * top_count
        grads = jnp.concatenate([back_ref[slot_ref[first + k]] for k in range(top_count)], axis=1)
        wide = jnp.concatenate([tiles_ref[a, k] for k in range(top_count)], axis=1)
        out_ref[a] = lax.dot_general(
            grads, wide, (((1,), (1,)), ((), ())), preferred_element_type=jnp.float32
        )


def adjoint_of(slot_index, returned, tiles):
    atm_blocks, top_count, cells, _ = tiles.shape
    slots, channels, _ = returned.shape
    per_step = math.gcd(atm_blocks, 4)
    return pl.pallas_call(
        adjoint_kernel,
        out_shape=jax.ShapeDtypeStruct((atm_blocks, channels, cells), jnp.float32),
        grid_spec=pltpu.PrefetchScalarGridSpec(
            num_scalar_prefetch=1,
            grid=(atm_blocks // per_step,),
            in_specs=[
                pl.BlockSpec((slots, channels, cells), lambda s, _: (0, 0, 0)),
                pl.BlockSpec((per_step, top_count, cells, cells), lambda s, _: (s, 0, 0, 0)),
            ],
            out_specs=pl.BlockSpec((per_step, channels, cells), lambda s, _: (s, 0, 0)),
        ),
        compiler_params=pltpu.CompilerParams(vmem_limit_bytes=VMEM_BYTES),
    )(slot_index, returned, tiles)


def features_kernel(id_ref, state_at_ref, states_ref, slots_ref, feat_ref, total_ref):
    slots = slots_ref.shape[0]
    total_ref[...] = jnp.zeros_like(total_ref)
    batch = math.gcd(slots, 8)

    @pl.loop(0, slots // batch)
    def _(step):
        places = [step * batch + b for b in range(batch)]
        pieces = [
            jnp.dot(
                states_ref[state_at_ref[slot]], slots_ref[slot], preferred_element_type=jnp.float32
            ).astype(jnp.bfloat16)
            for slot in places
        ]
        for slot, piece in zip(places, pieces):
            total_ref[id_ref[slot]] += piece.astype(jnp.float32)

    feat_ref[...] = total_ref[0 : feat_ref.shape[0]].astype(jnp.bfloat16)


def features_of(states, tiles, state_at, ids, ocean_blocks):
    _, channels, cells = states.shape
    whole = pl.BlockSpec(memory_space=pltpu.VMEM)
    return pl.pallas_call(
        features_kernel,
        out_shape=jax.ShapeDtypeStruct((ocean_blocks, channels, cells), jnp.bfloat16),
        in_specs=[pl.BlockSpec(memory_space=pltpu.SMEM)] * 2 + [whole] * 2,
        out_specs=whole,
        scratch_shapes=[pltpu.VMEM((ocean_blocks + 1, channels, cells), jnp.float32)],
        compiler_params=pltpu.CompilerParams(vmem_limit_bytes=VMEM_BYTES),
    )(ids, state_at, states, tiles)


PARTS = 4
CHUNKS = 2
MESH = pl.DeviceIdType.MESH


def exchange_kernel(
    space_size,
    member_size,
    scale_in,
    scale_out,
    features_ref,
    mask_ref,
    goal_ref,
    w_in_ref,
    w_in_t_ref,
    w_out_t_ref,
    w_out_3_ref,
    all_ref,
    sums_ref,
    feat_ref,
    grads_ref,
    in_ref,
    pre_ref,
    act_ref,
    out_ref,
    team_box,
    partial,
    place_box,
    total,
    team_send,
    team_recv,
    place_send,
    place_recv,
    line_send,
    line_recv,
    pair_send,
    pair_recv,
    own_sem,
):
    space, member = lax.axis_index("space"), lax.axis_index("member")
    length = space_size // 2
    place, core = space // 2, space % 2
    size = feat_ref.shape[0] // PARTS

    teams = 2 * member_size
    team = member * 2 + core

    def mate(i):
        other = lax.rem(team + i, teams)
        return other, {"space": place * 2 + other % 2, "member": other // 2}

    def far(i):
        other = lax.rem(place + i, length)
        return other, {"space": other * 2 + core}

    barrier = pltpu.get_barrier_semaphore()
    for i in range(1, teams):
        pl.semaphore_signal(barrier, inc=1, device_id=mate(i)[1], device_id_type=MESH)
    for i in range(1, length):
        pl.semaphore_signal(barrier, inc=1, device_id=far(i)[1], device_id_type=MESH)
    pl.semaphore_wait(barrier, teams + length - 2)

    def team_copy(back, i, owner):
        other, device = mate(i)
        rows = pl.ds((owner if back else other) * length, length)
        return pltpu.make_async_remote_copy(
            src_ref=sums_ref.at[rows] if back else grads_ref.at[rows],
            dst_ref=sums_ref.at[rows] if back else team_box.at[i - 1],
            send_sem=team_send.at[back, i - 1],
            recv_sem=team_recv.at[back, i - 1],
            device_id=device,
            device_id_type=MESH,
        )

    def place_copy(back, i, owner):
        other, device = far(i)
        return pltpu.make_async_remote_copy(
            src_ref=total if back else partial.at[other],
            dst_ref=sums_ref.at[team * length + owner] if back else place_box.at[i - 1],
            send_sem=place_send.at[back, i - 1],
            recv_sem=place_recv.at[back, i - 1],
            device_id=device,
            device_id_type=MESH,
        )

    own_sum = pltpu.make_async_copy(total, sums_ref.at[team * length + place], own_sem.at[1])

    def sum_team():
        for i in range(1, teams):
            team_copy(0, i, team).wait_recv()
        value = grads_ref[pl.ds(team * length, length)]
        for i in range(1, teams):
            value += team_box[i - 1]
        partial[...] = value
        for i in range(1, length):
            place_copy(0, i, place).start()

    def sum_places():
        for i in range(1, length):
            place_copy(0, i, place).wait_recv()
        value = partial[place]
        for i in range(1, length):
            value += place_box[i - 1]
        total[...] = value
        for i in range(1, length):
            place_copy(1, i, place).start()
        own_sum.start()

    def share_sums():
        for i in range(1, length):
            place_copy(1, i, far(length - i)[0]).wait_recv()
        own_sum.wait()
        for i in range(1, teams):
            team_copy(1, i, team).start()

    phases = [sum_team, sum_places, share_sums]

    def source(origin, own, c):
        rows = pl.ds(c * size, size)
        return feat_ref.at[rows] if own else all_ref.at[origin, rows]

    def line(way, hop, c, origin, own):
        step = 1 if way == 0 else -1
        return pltpu.make_async_remote_copy(
            src_ref=source(origin, own, c),
            dst_ref=all_ref.at[origin, pl.ds(c * size, size)],
            send_sem=line_send.at[way, hop, c],
            recv_sem=line_recv.at[way, hop, c],
            device_id={"space": (place + step) * 2 + core},
            device_id_type=MESH,
        )

    def pair(index, c, origin, own):
        return pltpu.make_async_remote_copy(
            src_ref=source(origin, own, c),
            dst_ref=all_ref.at[origin, pl.ds(c * size, size)],
            send_sem=pair_send.at[index, c],
            recv_sem=pair_recv.at[index, c],
            device_id={"space": place * 2 + 1 - core},
            device_id_type=MESH,
        )

    def behind(way, hop):
        at = place - 1 - hop if way == 0 else place + 1 + hop
        return at, (at >= 0 if way == 0 else at < length)

    ahead = (place < length - 1, place > 0)
    own_copy = pltpu.make_async_copy(feat_ref, all_ref.at[space], own_sem.at[0])
    hidden, channels = w_in_t_ref.shape
    cells = feat_ref.shape[2]
    group = math.gcd(size, 4)
    chunk = math.gcd(hidden, 256)
    in_ref[...] = jnp.zeros_like(in_ref)
    out_ref[...] = jnp.zeros_like(out_ref)

    @pl.loop(0, PARTS)
    def _(c):
        @pl.loop(c * (size // group), (c + 1) * (size // group))
        def _(step):
            first = step * group
            feat = jnp.concatenate(
                [features_ref[first + g] for g in range(group)], axis=1
            )
            predicted = jnp.zeros((8, group * cells), jnp.float32)
            for h in range(0, hidden, chunk):
                rows = slice(h, h + chunk)
                pre = jnp.dot(w_in_t_ref[rows], feat, preferred_element_type=jnp.float32)
                pre_ref[rows] = pre
                act = (pre * jax.nn.sigmoid(pre)).astype(jnp.bfloat16)
                act_ref[rows] = act
                predicted += jnp.dot(w_out_t_ref[:, rows], act, preferred_element_type=jnp.float32)
            goal = jnp.concatenate([goal_ref[first + g] for g in range(group)], axis=1)
            mask = jnp.concatenate([mask_ref[first + g] for g in range(group)], axis=1)
            misfit = mask * (predicted - goal)
            high = misfit.astype(jnp.bfloat16).astype(jnp.float32)
            rest = misfit - high
            middle = rest.astype(jnp.bfloat16).astype(jnp.float32)
            low = rest - middle
            misfit_3 = jnp.concatenate([high, middle, low, jnp.zeros_like(low)], axis=0).astype(
                jnp.bfloat16
            )
            feat_grad = jnp.zeros((channels, group * cells), jnp.float32)
            for h in range(0, hidden, chunk):
                rows = slice(h, h + chunk)
                act_grad = jnp.dot(w_out_3_ref[rows], misfit_3, preferred_element_type=jnp.float32)
                pre = pre_ref[rows]
                gate = jax.nn.sigmoid(pre)
                pre_grad = (act_grad * gate * (1.0 + pre * (1.0 - gate))).astype(jnp.bfloat16)
                feat_grad += jnp.dot(w_in_ref[:, rows], pre_grad, preferred_element_type=jnp.float32)
                in_ref[:, rows] += lax.dot_general(
                    feat, pre_grad, (((1,), (1,)), ((), ())), preferred_element_type=jnp.float32
                )
                out_ref[:, rows] += lax.dot_general(
                    misfit_3, act_ref[rows], (((1,), (1,)), ((), ())), preferred_element_type=jnp.float32
                )
            for g in range(group):
                feat_ref[first + g] = feat_grad[:, g * cells : (g + 1) * cells].astype(jnp.bfloat16)

        for way in range(2):

            @pl.when(ahead[way])
            def _():
                line(way, 0, c, space, True).start()

        pair(0, c, space, True).start()

    out = scale_out * (out_ref[0:8] + out_ref[8:16] + out_ref[16:24])
    for p in range(grads_ref.shape[0]):
        grads_ref[p, :, 0:hidden] = scale_in * in_ref[8 * p : 8 * p + 8]
        if (p + 1) * 128 <= hidden:
            grads_ref[p, :, hidden : hidden + 128] = out[:, p * 128 : (p + 1) * 128]
        else:
            grads_ref[p, :, hidden : hidden + 128] = jnp.zeros((8, 128), jnp.float32)

    for i in range(1, teams):
        team_copy(0, i, team).start()
    own_copy.start()

    for hop in range(length - 1):
        for c in range(PARTS):
            for way in range(2):
                at, there = behind(way, hop)
                origin = at * 2 + core

                @pl.when(there)
                def _():
                    line(way, hop, c, origin, False).wait_recv()
                    if hop + 1 < length - 1:

                        @pl.when(ahead[way])
                        def _():
                            line(way, hop + 1, c, origin, False).start()

                    pair(1 + way * (length - 1) + hop, c, origin, False).start()

            if phases:
                phases.pop(0)()

    own_copy.wait()
    for back in range(2):
        for i in range(1, teams):
            team_copy(back, i, team).wait_send()
        for i in range(1, length):
            place_copy(back, i, place).wait_send()
    for i in range(1, teams):
        team_copy(1, i, mate(teams - i)[0]).wait_recv()
    for c in range(PARTS):
        pair(0, c, space, True).wait_send()
        pair(0, c, place * 2 + 1 - core, False).wait_recv()
        for way in range(2):

            @pl.when(ahead[way])
            def _():
                line(way, 0, c, space, True).wait_send()

            for hop in range(length - 1):
                at, there = behind(way, hop)
                origin = at * 2 + core
                index = 1 + way * (length - 1) + hop

                @pl.when(there)
                def _():
                    if hop + 1 < length - 1:

                        @pl.when(ahead[way])
                        def _():
                            line(way, hop + 1, c, origin, False).wait_send()

                    pair(index, c, origin, False).wait_send()
                    pair(index, c, at * 2 + 1 - core, False).wait_recv()


def exchange(
    features, wet_mask, target, w_in, w_out, scale_in, scale_out, space_size, member_size
):
    ocean_blocks, channels, cells = features.shape
    hidden, outputs = w_out.shape
    group = math.gcd(ocean_blocks // PARTS, 4)
    padded = jnp.pad(w_out, ((0, 0), (0, 8 - outputs)))
    teams, length = 2 * member_size, space_size // 2
    hops = length - 1
    piece = (8, hidden + 128)
    dma = pltpu.SemaphoreType.DMA
    anywhere = pl.BlockSpec(memory_space=pl.ANY)
    return pl.pallas_call(
        lambda *refs: exchange_kernel(space_size, member_size, scale_in, scale_out, *refs),
        out_shape=(
            jax.ShapeDtypeStruct((space_size,) + features.shape, features.dtype),
            jax.ShapeDtypeStruct((channels // 8,) + piece, jnp.float32),
        ),
        in_specs=[pl.BlockSpec(memory_space=pltpu.VMEM)] * 7,
        out_specs=(anywhere, anywhere),
        scratch_shapes=[
            pltpu.VMEM(features.shape, features.dtype),
            pltpu.VMEM((channels // 8,) + piece, jnp.float32),
            pltpu.VMEM((channels, hidden), jnp.float32),
            pltpu.VMEM((hidden, group * cells), jnp.float32),
            pltpu.VMEM((hidden, group * cells), jnp.bfloat16),
            pltpu.VMEM((32, hidden), jnp.float32),
            pltpu.VMEM((teams - 1, length) + piece, jnp.float32),
            pltpu.VMEM((length,) + piece, jnp.float32),
            pltpu.VMEM((length - 1,) + piece, jnp.float32),
            pltpu.VMEM(piece, jnp.float32),
            dma((2, teams - 1)),
            dma((2, teams - 1)),
            dma((2, length - 1)),
            dma((2, length - 1)),
            dma((2, hops, PARTS)),
            dma((2, hops, PARTS)),
            dma((1 + 2 * hops, PARTS)),
            dma((1 + 2 * hops, PARTS)),
            dma((2,)),
        ],
        compiler_params=pltpu.CompilerParams(
            collective_id=0, has_side_effects=True, vmem_limit_bytes=VMEM_BYTES
        ),
    )(
        features,
        wet_mask.astype(jnp.float32)[:, None, :],
        jnp.pad(target, ((0, 0), (0, 8 - outputs), (0, 0))),
        w_in,
        w_in.T,
        padded.T,
        jnp.concatenate([padded, padded, padded, jnp.zeros_like(padded)], axis=1),
    )


def spread_kernel(
    space_size,
    columns,
    member_size,
    state_ref,
    tiles_ref,
    codes_ref,
    states_ref,
    slots_ref,
    all_codes_ref,
    code_send,
    code_recv,
    tile_send,
    tile_recv,
    share_send,
    share_recv,
    line_send,
    line_recv,
    pair_send,
    pair_recv,
    own_sem,
):
    group, space, member = (lax.axis_index(name) for name in ("group", "space", "member"))
    column = group * member_size + member
    length = space_size // 2
    place, core = space // 2, space % 2
    size = state_ref.shape[0] // CHUNKS
    share = tiles_ref.shape[1]

    def along(j):
        return lax.rem(space + j, space_size)

    def across(i):
        other = lax.rem(column + i, columns)
        return other, {"group": other // member_size, "member": other % member_size}

    barrier = pltpu.get_barrier_semaphore()
    for j in range(1, space_size):
        pl.semaphore_signal(barrier, inc=1, device_id={"space": along(j)}, device_id_type=MESH)
    for i in range(1, columns):
        pl.semaphore_signal(barrier, inc=1, device_id=across(i)[1], device_id_type=MESH)
    pl.semaphore_wait(barrier, space_size + columns - 2)

    def part(origin, owner):
        return slots_ref.at[origin, pl.ds(owner * share, share)]

    def tile(j, origin):
        return pltpu.make_async_remote_copy(
            src_ref=tiles_ref.at[along(j)],
            dst_ref=part(origin, column),
            send_sem=tile_send.at[j - 1],
            recv_sem=tile_recv.at[j - 1],
            device_id={"space": along(j)},
            device_id_type=MESH,
        )

    def code(j, origin):
        return pltpu.make_async_remote_copy(
            src_ref=codes_ref.at[along(j)],
            dst_ref=all_codes_ref.at[origin],
            send_sem=code_send.at[j - 1],
            recv_sem=code_recv.at[j - 1],
            device_id={"space": along(j)},
            device_id_type=MESH,
        )

    def shared(i, j, owner):
        origin = along(space_size - j)
        return pltpu.make_async_remote_copy(
            src_ref=tiles_ref.at[space] if j == 0 else part(origin, column),
            dst_ref=part(origin, owner),
            send_sem=share_send.at[i - 1, j],
            recv_sem=share_recv.at[i - 1, j],
            device_id=across(i)[1],
            device_id_type=MESH,
        )

    def source(origin, own, c):
        rows = pl.ds(c * size, size)
        return state_ref.at[rows] if own else states_ref.at[origin, rows]

    def line(way, hop, c, origin, own):
        step = 1 if way == 0 else -1
        return pltpu.make_async_remote_copy(
            src_ref=source(origin, own, c),
            dst_ref=states_ref.at[origin, pl.ds(c * size, size)],
            send_sem=line_send.at[way, hop, c],
            recv_sem=line_recv.at[way, hop, c],
            device_id={"space": (place + step) * 2 + core},
            device_id_type=MESH,
        )

    def pair(index, c, origin, own):
        return pltpu.make_async_remote_copy(
            src_ref=source(origin, own, c),
            dst_ref=states_ref.at[origin, pl.ds(c * size, size)],
            send_sem=pair_send.at[index, c],
            recv_sem=pair_recv.at[index, c],
            device_id={"space": place * 2 + 1 - core},
            device_id_type=MESH,
        )

    def behind(way, hop):
        at = place - 1 - hop if way == 0 else place + 1 + hop
        return at, (at >= 0 if way == 0 else at < length)

    ahead = (place < length - 1, place > 0)
    order = sorted(range(1, space_size), key=lambda j: min(j, space_size - j))
    for j in order:
        code(j, space).start()
        tile(j, space).start()
    own_codes = pltpu.make_async_copy(codes_ref.at[space], all_codes_ref.at[space], own_sem.at[2])
    own_codes.start()
    own_state = pltpu.make_async_copy(state_ref, states_ref.at[space], own_sem.at[0])
    own_tiles = pltpu.make_async_copy(tiles_ref.at[space], part(space, column), own_sem.at[1])
    for i in range(1, columns):
        shared(i, 0, column).start()
    for c in range(CHUNKS):
        for way in range(2):

            @pl.when(ahead[way])
            def _():
                line(way, 0, c, space, True).start()

        pair(0, c, space, True).start()
    own_state.start()
    own_tiles.start()

    hops = length - 1
    for hop in range(hops):
        for j in order[hop * len(order) // hops : (hop + 1) * len(order) // hops]:
            tile(j, along(space_size - j)).wait_recv()
            for i in range(1, columns):
                shared(i, j, column).start()
        for c in range(CHUNKS):
            for way in range(2):
                at, there = behind(way, hop)
                origin = at * 2 + core

                @pl.when(there)
                def _():
                    line(way, hop, c, origin, False).wait_recv()
                    if hop + 1 < hops:

                        @pl.when(ahead[way])
                        def _():
                            line(way, hop + 1, c, origin, False).start()

                    pair(1 + way * hops + hop, c, origin, False).start()

    own_state.wait()
    own_tiles.wait()
    own_codes.wait()
    for j in range(1, space_size):
        code(j, along(space_size - j)).wait_recv()
        code(j, space).wait_send()
        tile(j, space).wait_send()
    for i in range(1, columns):
        for j in range(space_size):
            shared(i, j, across(columns - i)[0]).wait_recv()
            shared(i, j, column).wait_send()
    for c in range(CHUNKS):
        pair(0, c, space, True).wait_send()
        pair(0, c, place * 2 + 1 - core, False).wait_recv()
        for way in range(2):

            @pl.when(ahead[way])
            def _():
                line(way, 0, c, space, True).wait_send()

            for hop in range(hops):
                at, there = behind(way, hop)
                origin = at * 2 + core
                index = 1 + way * hops + hop

                @pl.when(there)
                def _():
                    if hop + 1 < hops:

                        @pl.when(ahead[way])
                        def _():
                            line(way, hop + 1, c, origin, False).wait_send()

                    pair(index, c, origin, False).wait_send()
                    pair(index, c, at * 2 + 1 - core, False).wait_recv()


def spread(state, tile_slots, codes, space_size, columns, member_size):
    hops = space_size // 2 - 1
    _, share, cells, _ = tile_slots.shape
    dma = pltpu.SemaphoreType.DMA
    anywhere = pl.BlockSpec(memory_space=pl.ANY)
    return pl.pallas_call(
        lambda *refs: spread_kernel(space_size, columns, member_size, *refs),
        out_shape=(
            jax.ShapeDtypeStruct((space_size,) + state.shape, state.dtype),
            jax.ShapeDtypeStruct((space_size, columns * share, cells, cells), tile_slots.dtype),
            jax.ShapeDtypeStruct(codes.shape, codes.dtype),
        ),
        in_specs=[anywhere] * 3,
        out_specs=(anywhere,) * 3,
        scratch_shapes=[
            dma((space_size - 1,)),
            dma((space_size - 1,)),
            dma((space_size - 1,)),
            dma((space_size - 1,)),
            dma((columns - 1, space_size)),
            dma((columns - 1, space_size)),
            dma((2, hops, CHUNKS)),
            dma((2, hops, CHUNKS)),
            dma((1 + 2 * hops, CHUNKS)),
            dma((1 + 2 * hops, CHUNKS)),
            dma((3,)),
        ],
        compiler_params=pltpu.CompilerParams(
            collective_id=1, has_side_effects=True, vmem_limit_bytes=VMEM_BYTES
        ),
    )(state, tile_slots, codes)


def fused_body(atm_state, remap_tiles, dest_device, dest_block, wet_mask, target, w_in, w_out):
    space_size = lax.axis_size("space")
    member_size = lax.axis_size("member")
    atm_blocks, top_count, cells, _ = remap_tiles.shape
    ocean_blocks = wet_mask.shape[0]
    channels = atm_state.shape[2]
    pieces_fit = channels == 8 * space_size * member_size and w_in.shape[1] <= 16 * channels
    columns = lax.axis_size("group") * member_size
    capacity = min(atm_blocks, max(2, 2 * atm_blocks * top_count // space_size))
    if not pieces_fit or ocean_blocks % PARTS or atm_blocks % CHUNKS or capacity % columns:
        return general_body(
            atm_state, remap_tiles, dest_device, dest_block, wet_mask, target, w_in, w_out
        )
    pair_count = atm_blocks * top_count
    slot_total = space_size * capacity
    dest_flat = dest_device.reshape(pair_count)
    onehot = (dest_flat[:, None] == jnp.arange(space_size, dtype=jnp.int32)[None, :]).astype(
        jnp.int32
    )
    slot_rank = jnp.sum((jnp.cumsum(onehot, axis=0) - onehot) * onehot, axis=1)
    slot_index = dest_flat * capacity + slot_rank
    codes = (
        jnp.full((slot_total,), ocean_blocks * pair_count, jnp.int32)
        .at[slot_index]
        .set(dest_block.reshape(pair_count) * pair_count + jnp.arange(pair_count, dtype=jnp.int32))
    ).reshape(space_size, capacity)
    share = capacity // columns
    column = lax.axis_index("group") * member_size + lax.axis_index("member")
    mine = lax.dynamic_slice_in_dim(codes, column * share, share, axis=1)
    tile_slots = slotted_tiles(
        (mine % pair_count).reshape(-1), remap_tiles.reshape(pair_count, cells, cells)
    ).reshape(space_size, share, cells, cells)
    wide_codes = jnp.broadcast_to(
        jnp.pad(codes, ((0, 0), (0, -capacity % 128)))[:, None, :], (space_size, 8, -(-capacity // 128) * 128)
    )
    states, tiles, received_codes = spread(
        atm_state[0], tile_slots, wide_codes, space_size, columns, member_size
    )
    received_codes = received_codes[:, 0, :capacity]
    received_ids = (received_codes // pair_count).reshape(slot_total)
    state_at = (
        jnp.arange(space_size, dtype=jnp.int32)[:, None] * atm_blocks
        + received_codes % pair_count // top_count
    ).reshape(slot_total)
    cell_total = member_size * space_size * ocean_blocks * cells
    scale_in = math.sqrt(w_in.shape[1] / cell_total)
    scale_out = 1.0 / math.sqrt(cell_total)
    features = features_of(
        states.reshape(space_size * atm_blocks, channels, cells),
        tiles.reshape(slot_total, cells, cells),
        state_at,
        received_ids,
        ocean_blocks,
    )
    gathered, summed = exchange(
        features, wet_mask, target[0], w_in, w_out, scale_in, scale_out, space_size, member_size
    )
    owner = dest_flat * ocean_blocks + dest_block.reshape(pair_count)
    adjoint = adjoint_of(
        owner, gathered.reshape(space_size * ocean_blocks, channels, cells), remap_tiles
    )
    hidden, outputs = w_out.shape
    grad_in = summed[:, :, :hidden].reshape(channels, hidden)
    grad_out = summed[: hidden // 128, :outputs, hidden:]
    return (adjoint[None], grad_in, grad_out.transpose(0, 2, 1).reshape(hidden, outputs))


def solution(mesh):
    body = fused_body if mesh.shape["level"] == 1 and mesh.shape["space"] in (6, 8) else general_body
    return jax.shard_map(
        body,
        mesh=mesh,
        in_specs=(
            P("member", ("group", "space"), None, None),
            P("space", None, None, None),
            P("space", None),
            P("space", None),
            P("space", None),
            P("member", ("group", "space"), None, None),
            P(None, "level"),
            P("level", None),
        ),
        out_specs=(
            P("member", ("group", "space"), "level", None),
            P("group", "level"),
            P("level", "group"),
        ),
        check_vma=False,
    )
```
